128 devices in a mesh: ex: 16 (over x_hi, z, core), lay: 8 (over y, x_lo).
Axes of the slice: x: 4 (x_hi: 2, x_lo: 2; x = x_hi * 2 + x_lo), y: 4, z: 4, core: 2. Of those that a mesh axis runs over, the one named last changes fastest.
Arguments:
- training_gradient_rows: bfloat16 [8192, 16, 4096], P('ex', 'lay'), may hold values from -0.08984375 to 0.08984375
- test_grads: bfloat16 [2048, 16, 4096], P('ex', 'lay'), may hold values from -6 to 6
- inv_out: float32 [16, 64, 64], P('lay'), may hold values from -0.75 to 0.75
- inv_in: float32 [16, 64, 64], P('lay'), may hold values from -0.75 to 0.75
Outputs:
- scores: float32 [2048, 8192], P('lay', 'ex')
The draws below stay inside these ranges and needn't reach their ends.
All inputs are finite; a program needn't handle non-finite values.
Results may differ from the reference program's by a relative error of at most 0.015.
Values may be sent and summed in bfloat16 or wider, within the bound.
A program may use at most 128 MiB of HBM per device.

```python
import jax
import jax.numpy as jnp
from jax import lax

R = 64
PROJ = 4096
LAYER_DEV = 2
LAYERS = 16
TRAIN = 8192
TEST = 2048


def raised(values, own_key, source, target, parts, factor):
    owner, partner = [(jnp.arange(values.shape[axis_at]) // (values.shape[axis_at] // parts)).reshape([-1 if axis == axis_at else 1 for axis in range(values.ndim)]) for axis_at in (source, target)]
    chosen = jax.random.permutation(own_key, parts)[partner]
    strong = (owner == chosen) | (owner == (partner + parts // 2) % parts)
    return jnp.where(strong, factor * values, values)


def block_scale(stream_key, shape, shards, smallest, high):
    gain = 1.0
    for position, parts in shards:
        heights = jax.random.uniform(jax.random.fold_in(jax.random.fold_in(stream_key, 6), position), (parts,), jnp.float32, smallest / len(shards), high / len(shards))
        gain = gain * jnp.repeat(jnp.exp(heights), shape[position] // parts).reshape((-1,) + (1,) * (len(shape) - 1 - position))
    return gain


def bell_draw(own_key, dims, deviation, reach, pieces=(), held_as=jnp.bfloat16):
    entries = deviation * jax.random.normal(own_key, dims, jnp.float32)
    if pieces:
        entries = entries * block_scale(own_key, dims, pieces, -0.22, 0.18)
    return jnp.clip(entries, -reach, reach).astype(held_as)


def noise_with(stream_key, shape, spread, limit, split, heavy, dtype=jnp.bfloat16):
    entries = spread * jax.random.normal(stream_key, shape, jnp.float32)
    if split:
        entries = entries * block_scale(stream_key, shape, split, -0.22, 0.18)
    return jnp.clip(raised(entries, jax.random.fold_in(stream_key, 3), *heavy), -limit, limit).astype(dtype)


def setup_inputs(seed: int = 0) -> dict:
    key_of = jax.random.split(jax.random.key(seed), 5)
    return {
        "training_gradient_rows": bell_draw(key_of[0], (TRAIN, LAYERS, PROJ), 0.015625, 0.08984375, ((0, 16), (1, 8))),
        "test_grads": noise_with(key_of[1], (TEST, LAYERS, PROJ), 1.0, 6.0, ((0, 16), (1, 8)), (1, 0, 16, 2.0)),
        "inv_out": bell_draw(key_of[2], (LAYERS, R, R), R ** -0.5, 0.75, ((0, 8),), jnp.float32),
        "inv_in": bell_draw(key_of[3], (LAYERS, R, R), R ** -0.5, 0.75, ((0, 8),), jnp.float32),
    }


def reference(training_gradient_rows, test_grads, inv_out, inv_in):
    highest = lax.Precision.HIGHEST
    matrix_stack = test_grads.astype(jnp.float32).reshape(TEST, LAYERS, R, R)
    left = jnp.einsum('lab,tlbc->tlac', inv_out, matrix_stack, precision=highest)
    right = jnp.einsum('tlac,lcd->tlad', left, inv_in, precision=highest)
    precond = right.reshape(TEST, LAYERS, PROJ).astype(jnp.bfloat16)
    scores = jnp.zeros((TEST, TRAIN), jnp.float32)
    for group in range(LAYERS // LAYER_DEV):
        group_sum = jnp.zeros((TEST, TRAIN), jnp.float32)
        for inner in range(LAYER_DEV):
            layer = group * LAYER_DEV + inner
            part = lax.dot_general(precond[:, layer, :], training_gradient_rows[:, layer, :], (((1,), (1,)), ((), ())), preferred_element_type=jnp.float32)
            rounded = lax.optimization_barrier(part.astype(jnp.bfloat16))
            group_sum = group_sum + rounded.astype(jnp.float32)
        group_round = lax.optimization_barrier(group_sum.astype(jnp.bfloat16))
        scores = scores + group_round.astype(jnp.float32)
    return scores
```

```python
import functools

import jax
import jax.numpy as jnp
from jax import lax
from jax.experimental import pallas as pl
from jax.experimental.pallas import tpu as pltpu
from jax.sharding import PartitionSpec as P

BF, F32 = jnp.bfloat16, jnp.float32
NT = (((1,), (1,)), ((), ()))
TN = (((0,), (0,)), ((), ()))
HIGHEST = lax.Precision.HIGHEST

SLOTS = ((0, 0), (1, 0), (0, 3), (0, 1), (1, 3), (1, 1), (0, 2), (1, 2))
PIECES = 8
HEAD = 32
ROWS = 16
STEPS = 6
TREE_STEP = 2
PART = 512


def iota(shape, dim):
    return lax.broadcasted_iota(jnp.int32, shape, dim)


def kernel(train, test, inv_out, inv_in, out, g1, g2, bmat, stage, amat, weight, cs, yr, xs, xr, ysum,
           r1, r1s, s1, r2, r2h, r2s, s2, ysem, ysend, xsem, xsend, local):
    ex, lay = lax.axis_index("ex"), lax.axis_index("lay")
    xh, z, c = ex // 8, (ex // 2) % 4, ex % 2
    y, xl = lay // 2, lay % 2

    def at(xh_, z_, c_):
        return (xh_ * 8 + z_ * 2 + c_, lay)

    zup, zdown = lax.rem(z + 1, 4), lax.rem(z + 3, 4)
    to_x, to_up, to_down, to_s = at(1 - xh, z, c), at(xh, zup, c), at(xh, zdown, c), at(xh, z, 1 - c)
    to_y = [(ex, lax.rem(y + d, 4) * 2 + xl) for d in (1, 2, 3)]
    to_xl = (ex, y * 2 + 1 - xl)

    def remote(src, dst, send, recv, device):
        return pltpu.make_async_remote_copy(src_ref=src, dst_ref=dst, send_sem=send, recv_sem=recv,
                                            device_id=device, device_id_type=pl.DeviceIdType.MESH)

    def arrived(ref, recv):
        remote(ref, ref, s1.at[0, 0], recv, to_x).wait_recv()

    def left(ref, send):
        remote(ref, ref, send, r1.at[0, 0], to_x).wait_send()

    def fetch(i):
        if i < 0:
            src = test.reshape(256, 4096)
        else:
            src = train.reshape(1024, 4096).at[pl.ds(i * 256, 256)]
        return pltpu.make_async_copy(src, stage.at[(i + 1) % 2], local.at[(i + 1) % 2])

    fetch(-1).start()
    fetch(0).start()
    barrier = pltpu.get_barrier_semaphore()
    for device in [to_x, to_up, to_down, to_s, to_xl] + to_y:
        pl.semaphore_signal(barrier, inc=1, device_id=device, device_id_type=pl.DeviceIdType.MESH)

    def split_layers(slot, write):
        ri, ci = iota((256, 256), 0), iota((256, 256), 1)
        order = (ci == 2 * (ri % 128) + ri // 128).astype(BF)

        @pl.loop(0, 8)
        def _(i):
            cols = pl.ds(pl.multiple_of(i * 512, 512), 512)
            write(cols, jnp.dot(order, stage[slot, :, cols], preferred_element_type=F32).astype(BF))

    def write_a(cols, value):
        amat[0, :, cols] = value[:128]
        amat[1, :, cols] = value[128:]

    fetch(-1).wait()
    split_layers(0, write_a)
    fetch(1).start()
    pl.semaphore_wait(barrier, 8)

    def precondition(l, j):
        r, col = iota((64, PART), 0), iota((64, PART), 1)
        e = lax.dot_general(inv_out[l], (r == (PART // 64) * j + col // 64).astype(F32), TN,
                            precision=HIGHEST, preferred_element_type=F32)
        f = jnp.dot(inv_in[l], (r == col % 64).astype(F32), precision=HIGHEST, preferred_element_type=F32)
        weight[...] = (e[:, None, :] * f[None]).astype(BF).reshape(4096, PART)
        return jnp.dot(amat[l], weight[...], preferred_element_type=F32).astype(BF)

    def own1(p):
        ref = g1.at[p, 0]
        remote(ref, g1.at[p, 1], s1.at[p, 0], r1.at[p, 1], to_x).start()
        remote(ref, g1.at[p, 2], s1.at[p, 1], r1.at[p, 2], to_up).start()
        remote(ref, g1.at[p, 3], s1.at[p, 2], r1.at[p, 3], to_down).start()

    def first1(p):
        h = lax.rem(p, 2)
        arrived(g1.at[p, 1], r1.at[p, 1])
        remote(g1.at[p, 1], g1.at[p, 4], s1.at[p, 3], r1.at[p, 4], to_up).start()
        remote(g1.at[p, 1], g1.at[p, 5], s1.at[p, 4], r1.at[p, 5], to_down).start()
        arrived(g1.at[p, 2], r1.at[p, 2])
        arrived(g1.at[p, 3], r1.at[p, 3])
        onward = (jnp.where(h == 0, to_up[0], to_down[0]), lay)
        remote(g1.at[p, 2 + h], g1.at[p, 6], s1.at[p, 5], r1.at[p, 6], onward).start()
        remote(g1.at[p, pl.ds(0, 4)], g1.at[p, pl.ds(8, 4)], s1.at[p, 6], r1s.at[p, 0], to_s).start()

    def second1(p):
        arrived(g1.at[p, 6], r1.at[p, 6])
        remote(g1.at[p, 6], g1.at[p, 7], s1.at[p, 7], r1.at[p, 7], to_x).start()
        arrived(g1.at[p, 4], r1.at[p, 4])
        arrived(g1.at[p, 5], r1.at[p, 5])

    def third1(p):
        arrived(g1.at[p, 7], r1.at[p, 7])
        remote(g1.at[p, pl.ds(4, 4)], g1.at[p, pl.ds(12, 4)], s1.at[p, 8], r1s.at[p, 1], to_s).start()

    def drain1(p):
        for k in (0, 1, 2, 3, 4, 5, 7):
            left(g1.at[p, 0], s1.at[p, k])
        for k, group in ((6, 0), (8, 1)):
            left(g1.at[p, pl.ds(0, 4)], s1.at[p, k])
            arrived(g1.at[p, pl.ds(8 + 4 * group, 4)], r1s.at[p, group])

    def own2(i):
        ref = g2.at[i, 0]
        remote(ref, g2.at[i, 1], s2.at[i, 0], r2.at[i, 1], to_x).start()
        remote(ref, g2.at[i, 2], s2.at[i, 1], r2.at[i, 2], to_up).start()
        remote(ref, g2.at[i, 3], s2.at[i, 2], r2.at[i, 3], to_down).start()

    def first2(i):
        tree = i == TREE_STEP
        arrived(g2.at[i, 1], r2.at[i, 1])

        @pl.when(jnp.logical_not(tree))
        def _():
            remote(g2.at[i, 1], g2.at[i, 4], s2.at[i, 3], r2.at[i, 4], to_up).start()
            remote(g2.at[i, 1], g2.at[i, 5], s2.at[i, 4], r2.at[i, 5], to_down).start()

        arrived(g2.at[i, 2], r2.at[i, 2])
        remote(g2.at[i, 2, 0], g2.at[i, 6, 0], s2.at[i, 5], r2h.at[i, 0, 0], to_up).start()
        arrived(g2.at[i, 3], r2.at[i, 3])
        remote(g2.at[i, 3, 1], g2.at[i, 6, 1], s2.at[i, 6], r2h.at[i, 0, 1], to_down).start()

        @pl.when(tree)
        def _():
            remote(g2.at[i, 2], g2.at[i, 4], s2.at[i, 3], r2.at[i, 4], to_x).start()
            remote(g2.at[i, 3], g2.at[i, 5], s2.at[i, 4], r2.at[i, 5], to_x).start()

        remote(g2.at[i, pl.ds(0, 4)], g2.at[i, pl.ds(8, 4)], s2.at[i, 7], r2s.at[i, 0], to_s).start()

    def second2(i):
        for h in (0, 1):
            arrived(g2.at[i, 6, h], r2h.at[i, 0, h])
            remote(g2.at[i, 6, h], g2.at[i, 7, h], s2.at[i, 8 + h], r2h.at[i, 1, h], to_x).start()
        arrived(g2.at[i, 4], r2.at[i, 4])
        arrived(g2.at[i, 5], r2.at[i, 5])

    def third2(i):
        for h in (0, 1):
            arrived(g2.at[i, 7, h], r2h.at[i, 1, h])
        remote(g2.at[i, pl.ds(4, 4)], g2.at[i, pl.ds(12, 4)], s2.at[i, 10], r2s.at[i, 1], to_s).start()

    def fourth2(i):
        for group in (0, 1):
            arrived(g2.at[i, pl.ds(8 + 4 * group, 4)], r2s.at[i, group])

    def drain2(i):
        for k in (0, 1, 2, 3, 4):
            left(g2.at[i, 0], s2.at[i, k])
        for k in (5, 6, 8, 9):
            left(g2.at[i, 0, 0], s2.at[i, k])
        for k in (7, 10):
            left(g2.at[i, pl.ds(0, 4)], s2.at[i, k])

    def post(q, scores):
        for p in range(2):
            for k, (dx, dz) in enumerate(SLOTS):
                sx, sz = (1 - xh if dx else xh), lax.rem(z + dz, 4)
                row = pl.multiple_of(lax.rem(sz, 2) * 32 + (1 - c if p else c) * 16, 16)
                n = p * 8 + k
                cs[q, sx * 2 + sz // 2, pl.ds(row, 16), :] = scores[n * 16 : n * 16 + 16].astype(BF)
        for d in (1, 2, 3):
            remote(cs.at[q, lax.rem(y + d, 4)], yr.at[q, d - 1], ysend.at[q, d - 1], ysem.at[q, d - 1],
                   to_y[d - 1]).start()

    def over_y(q):
        total = cs[q, y].astype(F32)
        for d in range(3):
            arrived(yr.at[q, d], ysem.at[q, d])
            total += yr[q, d].astype(F32)
        ysum[q] = total.reshape(2, 32, 512)
        xs[q] = ysum[q, 1 - xl].astype(BF)
        remote(xs.at[q], xr.at[q], xsend.at[q], xsem.at[q], to_xl).start()

    def over_x(q):
        arrived(xr.at[q], xsem.at[q])
        total = ysum[q, xl] + xr[q].astype(F32)
        for k in range(2):
            out[pl.ds(pl.multiple_of(k * 128 + q * 16, 16), 16), :] = total[k * 16 : k * 16 + 16]

    def main_head(q):
        rows = pl.ds(pl.multiple_of(q * 16, 16), 16)
        scores = None
        for p in range(PIECES):
            lhs = g1[p, :, rows, :].reshape(256, 1024)
            part = lax.dot_general(lhs, bmat[p % 2, :, (p // 2) * 1024 : (p // 2 + 1) * 1024], NT,
                                   preferred_element_type=F32)
            scores = part if scores is None else scores + part
        post(q, scores)

    def main_step(i):
        scores = lax.dot_general(g2[i, :, 0].reshape(256, 4096), bmat[0], NT, preferred_element_type=F32)
        scores += lax.dot_general(g2[i, :, 1].reshape(256, 4096), bmat[1], NT, preferred_element_type=F32)
        post(i + 2, scores)

    @pl.loop(0, PIECES)
    def _(p):
        l, quarter = lax.rem(p, 2), p // 2

        @pl.loop(0, 2)
        def _(part):
            j = quarter * 2 + part
            value = precondition(l, j)
            g1[p, 0, :, pl.ds(pl.multiple_of(part * PART, PART), PART)] = value[:HEAD]
            cols = pl.ds(pl.multiple_of(j * PART, PART), PART)
            for i in range(STEPS):
                g2[i, 0, l, :, cols] = value[HEAD + i * ROWS : HEAD + (i + 1) * ROWS]

        own1(p)

        @pl.when(p >= 1)
        def _():
            first1(p - 1)

        @pl.when(p >= 2)
        def _():
            second1(p - 2)

        @pl.when(p >= 3)
        def _():
            third1(p - 3)

    last = PIECES - 1
    own2(0)
    first1(last)
    second1(last - 1)
    third1(last - 2)
    own2(1)
    second1(last)
    third1(last - 1)
    third1(last)

    @pl.loop(0, STEPS + 6)
    def _(t):
        @pl.when((t >= 2) & (t < STEPS))
        def _():
            own2(t)

        @pl.when((t >= 1) & (t < STEPS + 1))
        def _():
            first2(t - 1)

        @pl.when(t < 4)
        def _():
            slot = lax.rem(t + 1, 2)

            def write_b(cols, value):
                rows = pl.ds(pl.multiple_of(t * 128, 128), 128)
                bmat[0, rows, cols] = value[:128]
                bmat[1, rows, cols] = value[128:]

            pltpu.make_async_copy(train.reshape(1024, 4096).at[pl.ds(0, 256)], stage.at[slot], local.at[slot]).wait()
            split_layers(slot, write_b)

            @pl.when(t < 2)
            def _():
                start = pl.multiple_of((t + 2) * 256, 256)
                pltpu.make_async_copy(train.reshape(1024, 4096).at[pl.ds(start, 256)], stage.at[slot],
                                      local.at[slot]).start()

        @pl.when((t >= 2) & (t < STEPS + 2))
        def _():
            second2(t - 2)

        @pl.when((t >= 3) & (t < STEPS + 3))
        def _():
            third2(t - 3)

        @pl.when(t == 2)
        def _():
            @pl.loop(0, PIECES)
            def _(p):
                drain1(p)

        @pl.when(t == 3)
        def _():
            main_head(0)
            main_head(1)

        @pl.when((t >= 4) & (t < STEPS + 4))
        def _():
            fourth2(t - 4)
            main_step(t - 4)

        @pl.when(t == 4)
        def _():
            over_y(0)
            over_y(1)

        @pl.when((t >= 5) & (t < STEPS + 5))
        def _():
            over_y(t - 3)

        @pl.when(t == 5)
        def _():
            over_x(0)
            over_x(1)

        @pl.when(t >= 6)
        def _():
            drain2(t - 6)
            over_x(t - 4)

    @pl.loop(0, 8)
    def _(q):
        for d in range(3):
            left(cs.at[q, d], ysend.at[q, d])
        left(xs.at[q], xsend.at[q])


def body(train, test, inv_out, inv_in):
    vmem, hbm = pl.BlockSpec(memory_space=pltpu.VMEM), pl.BlockSpec(memory_space=pl.ANY)
    dma = pltpu.SemaphoreType.DMA
    return pl.pallas_call(
        kernel,
        out_shape=jax.ShapeDtypeStruct((256, 512), F32),
        in_specs=[hbm, hbm, vmem, vmem],
        out_specs=vmem,
        scratch_shapes=[
            pltpu.VMEM((PIECES, 16, HEAD, 1024), BF),
            pltpu.VMEM((STEPS, 16, 2, ROWS, 4096), BF),
            pltpu.VMEM((2, 512, 4096), BF),
            pltpu.VMEM((2, 256, 4096), BF),
            pltpu.VMEM((2, 128, 4096), BF),
            pltpu.VMEM((4096, PART), BF),
            pltpu.VMEM((8, 4, 64, 512), BF),
            pltpu.VMEM((8, 3, 64, 512), BF),
            pltpu.VMEM((8, 32, 512), BF),
            pltpu.VMEM((8, 32, 512), BF),
            pltpu.VMEM((8, 2, 32, 512), F32),
            dma((PIECES, 8)),
            dma((PIECES, 2)),
            dma((PIECES, 9)),
            dma((STEPS, 8)),
            dma((STEPS, 2, 2)),
            dma((STEPS, 2)),
            dma((STEPS, 11)),
            dma((8, 3)),
            dma((8, 3)),
            dma((8,)),
            dma((8,)),
            dma((2,)),
        ],
        compiler_params=pltpu.CompilerParams(
            collective_id=0, has_side_effects=True, vmem_limit_bytes=62 * 2**20
        ),
        cost_estimate=pl.CostEstimate(flops=26 * 10**9, bytes_accessed=12 * 2**20, transcendentals=0),
    )(train, test, inv_out, inv_in)


def solution(mesh):
    return jax.shard_map(
        body,
        mesh=mesh,
        in_specs=(P("ex", "lay", None), P("ex", "lay", None), P("lay", None, None), P("lay", None, None)),
        out_specs=P("lay", "ex"),
        check_vma=False,
    )
```

```python
import jax
import jax.numpy as jnp
from jax import lax
from jax.experimental import pallas as pl
from jax.experimental.pallas import tpu as pltpu
from jax.sharding import PartitionSpec as P

BF, F32 = jnp.bfloat16, jnp.float32
NT = (((1,), (1,)), ((), ()))
TN = (((0,), (0,)), ((), ()))
HIGHEST = lax.Precision.HIGHEST

SLOTS = ((0, 0), (1, 0), (0, 3), (0, 1), (1, 3), (1, 1), (0, 2), (1, 2))
PIECES = 8
HEAD = 64
ROWS = 16
ITEMS = 8
QUEUE = 8
PART = 512
CUT1, CUT2 = 896, 3584
RING = 5


def iota(shape, dim):
    return lax.broadcasted_iota(jnp.int32, shape, dim)


def kernel(train, test, inv_out, inv_in, out, g1, g2, bmat, stage, amat, weight, cs, yr, xs, xr, ysum, zr, acc,
           r1, r1h, r1c, r1s, r2, r2h, r2c, r2s, s2, ysem, ysend, xsem, xsend, zsem, zsend, local):
    ex, lay = lax.axis_index("ex"), lax.axis_index("lay")
    xh, z, c = ex // 8, (ex // 2) % 4, ex % 2
    y, xl = lay // 2, lay % 2

    def at(xh_, z_, c_):
        return (xh_ * 8 + z_ * 2 + c_, lay)

    to_x, to_s = at(1 - xh, z, c), at(xh, z, 1 - c)
    to_up, to_down = at(xh, lax.rem(z + 1, 4), c), at(xh, lax.rem(z + 3, 4), c)
    others = [(d, f) for f in (0, 1) for d in range(4) if d or f]
    to_lay = {(d, f): (ex, lax.rem(y + d, 4) * 2 + (1 - xl if f else xl)) for d, f in others}

    def remote(src, dst, send, recv, device):
        return pltpu.make_async_remote_copy(src_ref=src, dst_ref=dst, send_sem=send, recv_sem=recv,
                                            device_id=device, device_id_type=pl.DeviceIdType.MESH)

    def arrived(ref, recv):
        remote(ref, ref, s2.at[0, 0], recv, to_x).wait_recv()

    def left(ref, send):
        remote(ref, ref, send, r1.at[0, 0], to_x).wait_send()

    def fetch(i):
        if i < 0:
            src = test.reshape(256, 4096)
        else:
            src = train.reshape(1024, 4096).at[pl.ds(i * 256, 256)]
        return pltpu.make_async_copy(src, stage.at[(i + 1) % 2], local.at[(i + 1) % 2])

    fetch(-1).start()
    fetch(0).start()
    barrier = pltpu.get_barrier_semaphore()
    for device in [to_x, to_up, to_down, to_s] + [to_lay[k] for k in others]:
        pl.semaphore_signal(barrier, inc=1, device_id=device, device_id_type=pl.DeviceIdType.MESH)

    def weigh(l, j):
        r, col = iota((64, PART), 0), iota((64, PART), 1)
        e = lax.dot_general(inv_out[l], (r == (PART // 64) * j + col // 64).astype(F32), TN,
                            precision=HIGHEST, preferred_element_type=F32)
        f = jnp.dot(inv_in[l], (r == col % 64).astype(F32), precision=HIGHEST, preferred_element_type=F32)
        weight[...] = (e[:, None, :] * f[None]).astype(BF).reshape(4096, PART)

    def precondition(l, quarter, part):
        j = quarter * 2 + part
        value = jnp.dot(amat[l], weight[...], preferred_element_type=F32).astype(BF)
        g1[quarter * 2 + l, 0, :, pl.ds(pl.multiple_of(part * PART, PART), PART)] = value[:HEAD]
        cols = pl.ds(pl.multiple_of(j * PART, PART), PART)
        for i in range(ITEMS // 2):
            g2[i * 2 + l, 0, :, cols] = value[HEAD + i * ROWS : HEAD + (i + 1) * ROWS]

    def split_layers(slot, write):
        ri, ci = iota((256, 256), 0), iota((256, 256), 1)
        order = (ci == 2 * (ri % 128) + ri // 128).astype(BF)

        @pl.loop(0, 8)
        def _(i):
            cols = pl.ds(pl.multiple_of(i * 512, 512), 512)
            write(cols, jnp.dot(order, stage[slot, :, cols], preferred_element_type=F32).astype(BF))

    def write_a(cols, value):
        amat[0, :, cols] = value[:128]
        amat[1, :, cols] = value[128:]

    def split_train(t):
        slot = lax.rem(t + 1, 2)

        def write_b(cols, value):
            rows = pl.ds(pl.multiple_of(t * 128, 128), 128)
            bmat[0, rows, cols] = value[:128]
            bmat[1, rows, cols] = value[128:]

        pltpu.make_async_copy(train.reshape(1024, 4096).at[pl.ds(0, 256)], stage.at[slot], local.at[slot]).wait()
        split_layers(slot, write_b)

        @pl.when(t < 2)
        def _():
            start = pl.multiple_of((t + 2) * 256, 256)
            pltpu.make_async_copy(train.reshape(1024, 4096).at[pl.ds(start, 256)], stage.at[slot],
                                  local.at[slot]).start()

    def prepare(p):
        l, quarter = lax.rem(p, 2), p // 2

        @pl.loop(0, 2)
        def _(part):
            weigh(l, quarter * 2 + part)
            precondition(l, quarter, part)

    half1 = [pl.ds(h * HEAD // 2, HEAD // 2) for h in (0, 1)]
    rows1, near1, far1 = pl.ds(0, HEAD), pl.ds(0, CUT1), pl.ds(CUT1, 1024 - CUT1)

    def own1(p):
        ref = g1.at[p, 0]
        remote(ref, g1.at[p, 2], s2.at[lax.rem(p, RING), 1], r1.at[p, 1], to_up).start()
        remote(ref, g1.at[p, 3], s2.at[lax.rem(p, RING), 2], r1.at[p, 2], to_down).start()
        remote(ref, g1.at[p, 1], s2.at[lax.rem(p, RING), 0], r1.at[p, 0], to_x).start()

    def first1(p):
        for h, device in ((0, to_up), (1, to_down)):
            arrived(g1.at[p, 2 + h], r1.at[p, 1 + h])
            remote(g1.at[p, 2 + h, half1[h]], g1.at[p, 6, half1[h]], s2.at[lax.rem(p, RING), 5 + h], r1h.at[p, 0, h], device).start()
            remote(g1.at[p, 2 + h, rows1, far1], g1.at[p, 4 + h, rows1, far1], s2.at[lax.rem(p, RING), 11 + h], r1c.at[p, h],
                   to_x).start()
        arrived(g1.at[p, 1], r1.at[p, 0])
        for h, device in ((0, to_up), (1, to_down)):
            remote(g1.at[p, 1, rows1, near1], g1.at[p, 4 + h, rows1, near1], s2.at[lax.rem(p, RING), 3 + h], r1.at[p, 3 + h],
                   device).start()
        remote(g1.at[p, pl.ds(0, 4)], g1.at[p, pl.ds(8, 4)], s2.at[lax.rem(p, RING), 7], r1s.at[p, 0], to_s).start()

    def second1(p):
        for h in (0, 1):
            arrived(g1.at[p, 6, half1[h]], r1h.at[p, 0, h])
            remote(g1.at[p, 6, half1[h]], g1.at[p, 7, half1[h]], s2.at[lax.rem(p, RING), 8 + h], r1h.at[p, 1, h], to_x).start()
        for h in (0, 1):
            arrived(g1.at[p, 4 + h, rows1, near1], r1.at[p, 3 + h])
            arrived(g1.at[p, 4 + h, rows1, far1], r1c.at[p, h])

    def third1(p):
        for h in (0, 1):
            arrived(g1.at[p, 7, half1[h]], r1h.at[p, 1, h])
        remote(g1.at[p, pl.ds(4, 4)], g1.at[p, pl.ds(12, 4)], s2.at[lax.rem(p, RING), 10], r1s.at[p, 1], to_s).start()

    def drain1(p):
        for k in (0, 1, 2):
            left(g1.at[p, 0], s2.at[lax.rem(p, RING), k])
        for k in (3, 4):
            left(g1.at[p, 0, rows1, near1], s2.at[lax.rem(p, RING), k])
        for k in (11, 12):
            left(g1.at[p, 0, rows1, far1], s2.at[lax.rem(p, RING), k])
        for k in (5, 6, 8, 9):
            left(g1.at[p, 0, half1[0]], s2.at[lax.rem(p, RING), k])
        for k, group in ((7, 0), (10, 1)):
            left(g1.at[p, pl.ds(0, 4)], s2.at[lax.rem(p, RING), k])

    half2 = [pl.ds(h * 2048, 2048) for h in (0, 1)]
    rows2, near2, far2 = pl.ds(0, ROWS), pl.ds(0, CUT2), pl.ds(CUT2, 4096 - CUT2)

    def own2(i):
        ref = g2.at[i, 0]
        remote(ref, g2.at[i, 2], s2.at[lax.rem(PIECES + i, RING), 1], r2.at[i, 1], to_up).start()
        remote(ref, g2.at[i, 3], s2.at[lax.rem(PIECES + i, RING), 2], r2.at[i, 2], to_down).start()
        remote(ref, g2.at[i, 1], s2.at[lax.rem(PIECES + i, RING), 0], r2.at[i, 0], to_x).start()

    def first2(i):
        for h, device in ((0, to_up), (1, to_down)):
            arrived(g2.at[i, 2 + h], r2.at[i, 1 + h])
            remote(g2.at[i, 2 + h, rows2, half2[h]], g2.at[i, 6, rows2, half2[h]], s2.at[lax.rem(PIECES + i, RING), 5 + h], r2h.at[i, 0, h],
                   device).start()
            remote(g2.at[i, 2 + h, rows2, far2], g2.at[i, 4 + h, rows2, far2], s2.at[lax.rem(PIECES + i, RING), 12 + h], r2c.at[i, h],
                   to_x).start()
        arrived(g2.at[i, 1], r2.at[i, 0])
        for h, device in ((0, to_up), (1, to_down)):
            remote(g2.at[i, 1, rows2, near2], g2.at[i, 4 + h, rows2, near2], s2.at[lax.rem(PIECES + i, RING), 3 + h], r2.at[i, 3 + h],
                   device).start()
        remote(g2.at[i, pl.ds(0, 4)], g2.at[i, pl.ds(8, 4)], s2.at[lax.rem(PIECES + i, RING), 7], r2s.at[i, 0], to_s).start()

    def second2(i):
        for h in (0, 1):
            arrived(g2.at[i, 6, rows2, half2[h]], r2h.at[i, 0, h])
            remote(g2.at[i, 6, rows2, half2[h]], g2.at[i, 7, rows2, half2[h]], s2.at[lax.rem(PIECES + i, RING), 8 + h], r2h.at[i, 1, h],
                   to_x).start()
        for h in (0, 1):
            arrived(g2.at[i, 4 + h, rows2, near2], r2.at[i, 3 + h])
            arrived(g2.at[i, 4 + h, rows2, far2], r2c.at[i, h])
        remote(g2.at[i, pl.ds(4, 3)], g2.at[i, pl.ds(12, 3)], s2.at[lax.rem(PIECES + i, RING), 10], r2s.at[i, 1], to_s).start()

    def third2(i):
        for h in (0, 1):
            arrived(g2.at[i, 7, rows2, half2[h]], r2h.at[i, 1, h])
        remote(g2.at[i, 7], g2.at[i, 15], s2.at[lax.rem(PIECES + i, RING), 11], r2s.at[i, 2], to_s).start()

    def from_sibling(i, groups):
        for group in groups:
            ref = g2.at[i, pl.ds(8, 4)] if group == 0 else g2.at[i, pl.ds(12, 3)] if group == 1 else g2.at[i, 15]
            arrived(ref, r2s.at[i, group])

    def drain2(i):
        for k in (0, 1, 2, 11):
            left(g2.at[i, 0], s2.at[lax.rem(PIECES + i, RING), k])
        for k in (3, 4):
            left(g2.at[i, 0, rows2, near2], s2.at[lax.rem(PIECES + i, RING), k])
        for k in (12, 13):
            left(g2.at[i, 0, rows2, far2], s2.at[lax.rem(PIECES + i, RING), k])
        for k in (5, 6, 8, 9):
            left(g2.at[i, 0, rows2, half2[0]], s2.at[lax.rem(PIECES + i, RING), k])
        left(g2.at[i, pl.ds(0, 4)], s2.at[lax.rem(PIECES + i, RING), 7])
        left(g2.at[i, pl.ds(4, 3)], s2.at[lax.rem(PIECES + i, RING), 10])

    def keep(q, slots, scores):
        for n, (p, k) in enumerate(slots):
            dx, dz = SLOTS[k]
            sx, sz = (1 - xh if dx else xh), lax.rem(z + dz, 4)
            row = pl.multiple_of(lax.rem(sz, 2) * 32 + (1 - c if p else c) * 16, 16)
            cs[lax.rem(q, 4), sx * 2 + sz // 2, pl.ds(row, 16), :] = scores[n * 16 : n * 16 + 16].astype(BF)

    every = [(p, k) for p in range(2) for k in range(8)]
    early = [(p, k) for p in range(2) for k in range(4)]
    late = [(p, k) for p in range(2) for k in range(4, 8)]

    def to_y(q):
        for d in (1, 2, 3):
            remote(cs.at[lax.rem(q, 4), lax.rem(y + d, 4)], yr.at[q, d - 1], ysend.at[lax.rem(q, 4), d - 1], ysem.at[q, d - 1],
                   to_lay[d, 0]).start()

    def over_y(q):
        total = cs[lax.rem(q, 4), y].astype(F32)
        for d in range(3):
            arrived(yr.at[q, d], ysem.at[q, d])
            left(yr.at[q, d], ysend.at[lax.rem(q, 4), d])
            total += yr[q, d].astype(F32)
        ysum[lax.rem(q, 4)] = total.reshape(2, 32, 512)
        xs[lax.rem(q, 4)] = ysum[lax.rem(q, 4), 1 - xl].astype(BF)
        remote(xs.at[lax.rem(q, 4)], xr.at[q], xsend.at[lax.rem(q, 4)], xsem.at[q], to_lay[0, 1]).start()

    def finish(q, total):
        for k in range(2):
            out[pl.ds(pl.multiple_of(k * 128 + q * 16, 16), 16), :] = total[k * 16 : k * 16 + 16]

    def over_x(q):
        arrived(xr.at[q], xsem.at[q])
        left(xr.at[q], xsend.at[lax.rem(q, 4)])
        finish(q, ysum[lax.rem(q, 4), xl] + xr[q].astype(F32))

    def main_head(q):
        rows = pl.ds(pl.multiple_of(q * 16, 16), 16)
        acc[1] = jnp.zeros((256, 512), F32)

        @pl.loop(0, PIECES // 2)
        def _(j):
            cols = pl.ds(pl.multiple_of(j * 1024, 1024), 1024)
            for l in (0, 1):
                lhs = g1[j * 2 + l, :, rows, :].reshape(256, 1024)
                acc[1] += lax.dot_general(lhs, bmat[l, :, cols], NT, preferred_element_type=F32)

        keep(q, every, acc[1])
        to_y(q)

    def product(l, lhs):
        return lax.dot_general(lhs, bmat[l], NT, preferred_element_type=F32)

    def main_item(n):
        l = lax.rem(n, 2)
        acc[0] = jnp.where(l == 0, jnp.zeros((256, 512), F32), acc[0]) + product(l, g2[n].reshape(256, 4096))

        @pl.when(l == 1)
        def _():
            q = HEAD // 16 + n // 2
            keep(q, every, acc[0])
            to_y(q)

    fetch(-1).wait()
    split_layers(0, write_a)
    fetch(1).start()
    prepare(0)
    pl.semaphore_wait(barrier, 11)

    end1, end2 = PIECES, PIECES + ITEMS

    @pl.loop(0, end2 + 3)
    def _(t):
        def during(start, stop, do, odd=None):
            on = (t >= start) & (t < stop)
            if odd is not None:
                on = on & (lax.rem(t, 2) == odd)
            pl.when(on)(do)

        def head_from_sibling():
            @pl.loop(0, PIECES)
            def _(p):
                for group in (0, 1):
                    arrived(g1.at[p, pl.ds(8 + 4 * group, 4)], r1s.at[p, group])


        during(RING, end1 + RING, lambda: drain1(t - RING))
        during(end1 + RING, end2 + RING, lambda: drain2(t - end1 - RING))
        during(0, end1, lambda: own1(t))
        during(end1, end2, lambda: own2(t - end1))
        during(1, end1 + 1, lambda: first1(t - 1))
        during(end1 + 1, end2 + 1, lambda: first2(t - end1 - 1))
        during(2, end1 + 2, lambda: second1(t - 2))
        during(end1 + 2, end2 + 2, lambda: second2(t - end1 - 2))
        during(0, end1 - 1, lambda: prepare(t + 1))
        during(0, end1, lambda: split_train(t // 2), 1)

        def item():
            from_sibling(t - end1 - 4, (0, 1, 2))
            main_item(t - end1 - 4)

        first_main = end1 + 3
        heads = HEAD // 16
        during(first_main, first_main + 1, head_from_sibling)
        during(first_main, first_main + heads, lambda: main_head(t - first_main))
        during(end1 + 4, end2 + 3, item)
        during(first_main + 1, first_main + 1 + heads, lambda: over_y(t - first_main - 1))
        during(end1 + 6, end2 + 3, lambda: over_y(heads + (t - end1 - 6) // 2), end1 % 2)
        during(first_main + 2, first_main + 2 + heads, lambda: over_x(t - first_main - 2))
        during(end1 + 7, end2 + 3, lambda: over_x(heads + (t - end1 - 7) // 2), 1 - end1 % 2)
        during(3, end1 + 3, lambda: third1(t - 3))
        during(end1 + 3, end2 + 2, lambda: third2(t - end1 - 3))

    i, q = ITEMS - 1, QUEUE - 1

    def last(k, slots):
        lhs = jnp.concatenate([g2[i, p + k : p + k + 4].reshape(64, 4096) for p in (0, 8)], axis=0)
        done = jnp.concatenate([acc[0, (p + k) * 16 : (p + k) * 16 + 64] for p in (0, 8)], axis=0)
        keep(q, slots, done + product(1, lhs))

    from_sibling(i, (0,))
    last(0, early)
    third2(i)

    from_sibling(i, (1, 2))
    last(4, late)
    mine = pl.ds(pl.multiple_of(xl * 32, 32), 32)
    yours = pl.ds(pl.multiple_of(32 - xl * 32, 32), 32)
    for n, (d, f) in enumerate(others):
        remote(cs.at[q % 4, lax.rem(y + d, 4), yours if f else mine], zr.at[n], zsend.at[n], zsem.at[n],
               to_lay[d, f]).start()
    for n in range(end2 + 3 - RING, end2):
        drain2(n - end1)
    total = cs[q % 4, y, mine, :].astype(F32)
    for n in range(len(others)):
        arrived(zr.at[n], zsem.at[n])
        total += zr[n].astype(F32)
    finish(q, total)
    over_x(q - 1)
    for n in range(len(others)):
        left(zr.at[n], zsend.at[n])


def body(train, test, inv_out, inv_in):
    vmem, hbm = pl.BlockSpec(memory_space=pltpu.VMEM), pl.BlockSpec(memory_space=pl.ANY)
    dma = pltpu.SemaphoreType.DMA
    return pl.pallas_call(
        kernel,
        out_shape=jax.ShapeDtypeStruct((256, 512), F32),
        in_specs=[hbm, hbm, vmem, vmem],
        out_specs=vmem,
        scratch_shapes=[
            pltpu.VMEM((PIECES, 16, HEAD, 1024), BF),
            pltpu.VMEM((ITEMS, 16, ROWS, 4096), BF),
            pltpu.VMEM((2, 512, 4096), BF),
            pltpu.VMEM((2, 256, 4096), BF),
            pltpu.VMEM((2, 128, 4096), BF),
            pltpu.VMEM((4096, PART), BF),
            pltpu.VMEM((4, 4, 64, 512), BF),
            pltpu.VMEM((QUEUE - 1, 3, 64, 512), BF),
            pltpu.VMEM((4, 32, 512), BF),
            pltpu.VMEM((QUEUE - 1, 32, 512), BF),
            pltpu.VMEM((4, 2, 32, 512), F32),
            pltpu.VMEM((7, 32, 512), BF),
            pltpu.VMEM((2, 256, 512), F32),
            dma((PIECES, 5)),
            dma((PIECES, 2, 2)),
            dma((PIECES, 2)),
            dma((PIECES, 2)),
            dma((ITEMS, 5)),
            dma((ITEMS, 2, 2)),
            dma((ITEMS, 2)),
            dma((ITEMS, 3)),
            dma((RING, 14)),
            dma((QUEUE - 1, 3)),
            dma((4, 3)),
            dma((QUEUE - 1,)),
            dma((4,)),
            dma((7,)),
            dma((7,)),
            dma((2,)),
        ],
        compiler_params=pltpu.CompilerParams(
            collective_id=0, has_side_effects=True, vmem_limit_bytes=62 * 2**20
        ),
        cost_estimate=pl.CostEstimate(flops=26 * 10**9, bytes_accessed=12 * 2**20, transcendentals=0),
    )(train, test, inv_out, inv_in)


def solution(mesh):
    return jax.shard_map(
        body,
        mesh=mesh,
        in_specs=(P("ex", "lay", None), P("ex", "lay", None), P("lay", None, None), P("lay", None, None)),
        out_specs=P("lay", "ex"),
        check_vma=False,
    )
```

```python
import jax
import jax.numpy as jnp
from jax import lax
from jax.experimental import pallas as pl
from jax.experimental.pallas import tpu as pltpu
from jax.sharding import PartitionSpec as P

BF, F32 = jnp.bfloat16, jnp.float32
NT = (((1,), (1,)), ((), ()))
TN = (((0,), (0,)), ((), ()))
HIGHEST = lax.Precision.HIGHEST

SLOTS = ((0, 0), (1, 0), (0, 3), (0, 1), (1, 3), (1, 1), (0, 2), (1, 2))
PIECES = 8
HEAD = 64
ROWS = 16
ITEMS = 8
QUEUE = 8
PART = 512
CUT1, CUT2 = 896, 3584
RING = 5


def iota(shape, dim):
    return lax.broadcasted_iota(jnp.int32, shape, dim)


def kernel(train, test, inv_out, inv_in, out, g1, g2, bmat, stage, amat, weight, cs, yr, xs, xr, ysum, zr, acc,
           r1, r1h, r1c, r1s, r2, r2h, r2c, r2s, s2, ysem, ysend, xsem, xsend, zsem, zsend, local):
    ex, lay = lax.axis_index("ex"), lax.axis_index("lay")
    xh, z, c = ex // 8, (ex // 2) % 4, ex % 2
    y, xl = lay // 2, lay % 2

    def at(xh_, z_, c_):
        return (xh_ * 8 + z_ * 2 + c_, lay)

    to_x, to_s = at(1 - xh, z, c), at(xh, z, 1 - c)
    to_up, to_down = at(xh, lax.rem(z + 1, 4), c), at(xh, lax.rem(z + 3, 4), c)
    others = [(d, f) for f in (0, 1) for d in range(4) if d or f]
    to_lay = {(d, f): (ex, lax.rem(y + d, 4) * 2 + (1 - xl if f else xl)) for d, f in others}

    def remote(src, dst, send, recv, device):
        return pltpu.make_async_remote_copy(src_ref=src, dst_ref=dst, send_sem=send, recv_sem=recv,
                                            device_id=device, device_id_type=pl.DeviceIdType.MESH)

    def arrived(ref, recv):
        remote(ref, ref, s2.at[0, 0], recv, to_x).wait_recv()

    def left(ref, send):
        remote(ref, ref, send, r1.at[0, 0], to_x).wait_send()

    def fetch(i):
        if i < 0:
            src = test.reshape(256, 4096)
        else:
            src = train.reshape(1024, 4096).at[pl.ds(i * 256, 256)]
        return pltpu.make_async_copy(src, stage.at[(i + 1) % 2], local.at[(i + 1) % 2])

    fetch(-1).start()
    fetch(0).start()
    barrier = pltpu.get_barrier_semaphore()
    for device in [to_x, to_up, to_down, to_s] + [to_lay[k] for k in others]:
        pl.semaphore_signal(barrier, inc=1, device_id=device, device_id_type=pl.DeviceIdType.MESH)

    def weigh(l, j):
        r, col = iota((64, PART), 0), iota((64, PART), 1)
        e = lax.dot_general(inv_out[l], (r == (PART // 64) * j + col // 64).astype(F32), TN,
                            precision=HIGHEST, preferred_element_type=F32)
        f = jnp.dot(inv_in[l], (r == col % 64).astype(F32), precision=HIGHEST, preferred_element_type=F32)
        weight[...] = (e[:, None, :] * f[None]).astype(BF).reshape(4096, PART)

    def precondition(l, quarter, part):
        j = quarter * 2 + part
        value = jnp.dot(amat[l], weight[...], preferred_element_type=F32).astype(BF)
        g1[quarter * 2 + l, 0, :, pl.ds(pl.multiple_of(part * PART, PART), PART)] = value[:HEAD]
        cols = pl.ds(pl.multiple_of(j * PART, PART), PART)
        for i in range(ITEMS // 2):
            g2[i * 2 + l, 0, :, cols] = value[HEAD + i * ROWS : HEAD + (i + 1) * ROWS]

    def split_layers(slot, write):
        ri, ci = iota((256, 256), 0), iota((256, 256), 1)
        order = (ci == 2 * (ri % 128) + ri // 128).astype(BF)

        @pl.loop(0, 8)
        def _(i):
            cols = pl.ds(pl.multiple_of(i * 512, 512), 512)
            write(cols, jnp.dot(order, stage[slot, :, cols], preferred_element_type=F32).astype(BF))

    def write_a(cols, value):
        amat[0, :, cols] = value[:128]
        amat[1, :, cols] = value[128:]

    def split_train(t):
        slot = lax.rem(t + 1, 2)

        def write_b(cols, value):
            rows = pl.ds(pl.multiple_of(t * 128, 128), 128)
            bmat[0, rows, cols] = value[:128]
            bmat[1, rows, cols] = value[128:]

        pltpu.make_async_copy(train.reshape(1024, 4096).at[pl.ds(0, 256)], stage.at[slot], local.at[slot]).wait()
        split_layers(slot, write_b)

        @pl.when(t < 2)
        def _():
            start = pl.multiple_of((t + 2) * 256, 256)
            pltpu.make_async_copy(train.reshape(1024, 4096).at[pl.ds(start, 256)], stage.at[slot],
                                  local.at[slot]).start()

    def prepare(p):
        l, quarter = lax.rem(p, 2), p // 2

        @pl.loop(0, 2)
        def _(part):
            weigh(l, quarter * 2 + part)
            precondition(l, quarter, part)

    half1 = [pl.ds(h * HEAD // 2, HEAD // 2) for h in (0, 1)]
    rows1, near1, far1 = pl.ds(0, HEAD), pl.ds(0, CUT1), pl.ds(CUT1, 1024 - CUT1)

    def own1(p):
        ref = g1.at[p, 0]
        remote(ref, g1.at[p, 2], s2.at[lax.rem(p, RING), 1], r1.at[p, 1], to_up).start()
        remote(ref, g1.at[p, 3], s2.at[lax.rem(p, RING), 2], r1.at[p, 2], to_down).start()
        remote(ref, g1.at[p, 1], s2.at[lax.rem(p, RING), 0], r1.at[p, 0], to_x).start()

    def first1(p):
        for h, device in ((0, to_up), (1, to_down)):
            arrived(g1.at[p, 2 + h], r1.at[p, 1 + h])
            remote(g1.at[p, 2 + h, half1[h]], g1.at[p, 6, half1[h]], s2.at[lax.rem(p, RING), 5 + h], r1h.at[p, 0, h], device).start()
            remote(g1.at[p, 2 + h, rows1, far1], g1.at[p, 4 + h, rows1, far1], s2.at[lax.rem(p, RING), 11 + h], r1c.at[p, h],
                   to_x).start()
        arrived(g1.at[p, 1], r1.at[p, 0])
        for h, device in ((0, to_up), (1, to_down)):
            remote(g1.at[p, 1, rows1, near1], g1.at[p, 4 + h, rows1, near1], s2.at[lax.rem(p, RING), 3 + h], r1.at[p, 3 + h],
                   device).start()
        remote(g1.at[p, pl.ds(0, 4)], g1.at[p, pl.ds(8, 4)], s2.at[lax.rem(p, RING), 7], r1s.at[p, 0], to_s).start()

    def second1(p):
        for h in (0, 1):
            arrived(g1.at[p, 6, half1[h]], r1h.at[p, 0, h])
            remote(g1.at[p, 6, half1[h]], g1.at[p, 7, half1[h]], s2.at[lax.rem(p, RING), 8 + h], r1h.at[p, 1, h], to_x).start()
        for h in (0, 1):
            arrived(g1.at[p, 4 + h, rows1, near1], r1.at[p, 3 + h])
            arrived(g1.at[p, 4 + h, rows1, far1], r1c.at[p, h])

    def third1(p):
        for h in (0, 1):
            arrived(g1.at[p, 7, half1[h]], r1h.at[p, 1, h])
        remote(g1.at[p, pl.ds(4, 4)], g1.at[p, pl.ds(12, 4)], s2.at[lax.rem(p, RING), 10], r1s.at[p, 1], to_s).start()

    def drain1(p):
        for k in (0, 1, 2):
            left(g1.at[p, 0], s2.at[lax.rem(p, RING), k])
        for k in (3, 4):
            left(g1.at[p, 0, rows1, near1], s2.at[lax.rem(p, RING), k])
        for k in (11, 12):
            left(g1.at[p, 0, rows1, far1], s2.at[lax.rem(p, RING), k])
        for k in (5, 6, 8, 9):
            left(g1.at[p, 0, half1[0]], s2.at[lax.rem(p, RING), k])
        for k, group in ((7, 0), (10, 1)):
            left(g1.at[p, pl.ds(0, 4)], s2.at[lax.rem(p, RING), k])

    half2 = [pl.ds(h * 2048, 2048) for h in (0, 1)]
    rows2, near2, far2 = pl.ds(0, ROWS), pl.ds(0, CUT2), pl.ds(CUT2, 4096 - CUT2)

    def own2(i):
        ref = g2.at[i, 0]
        remote(ref, g2.at[i, 2], s2.at[lax.rem(PIECES + i, RING), 1], r2.at[i, 1], to_up).start()
        remote(ref, g2.at[i, 3], s2.at[lax.rem(PIECES + i, RING), 2], r2.at[i, 2], to_down).start()
        remote(ref, g2.at[i, 1], s2.at[lax.rem(PIECES + i, RING), 0], r2.at[i, 0], to_x).start()

    def first2(i):
        for h, device in ((0, to_up), (1, to_down)):
            arrived(g2.at[i, 2 + h], r2.at[i, 1 + h])
            remote(g2.at[i, 2 + h, rows2, half2[h]], g2.at[i, 6, rows2, half2[h]], s2.at[lax.rem(PIECES + i, RING), 5 + h], r2h.at[i, 0, h],
                   device).start()
            remote(g2.at[i, 2 + h, rows2, far2], g2.at[i, 4 + h, rows2, far2], s2.at[lax.rem(PIECES + i, RING), 12 + h], r2c.at[i, h],
                   to_x).start()
        arrived(g2.at[i, 1], r2.at[i, 0])
        for h, device in ((0, to_up), (1, to_down)):
            remote(g2.at[i, 1, rows2, near2], g2.at[i, 4 + h, rows2, near2], s2.at[lax.rem(PIECES + i, RING), 3 + h], r2.at[i, 3 + h],
                   device).start()
        remote(g2.at[i, pl.ds(0, 4)], g2.at[i, pl.ds(8, 4)], s2.at[lax.rem(PIECES + i, RING), 7], r2s.at[i, 0], to_s).start()

    def second2(i):
        for h in (0, 1):
            arrived(g2.at[i, 6, rows2, half2[h]], r2h.at[i, 0, h])
            remote(g2.at[i, 6, rows2, half2[h]], g2.at[i, 7, rows2, half2[h]], s2.at[lax.rem(PIECES + i, RING), 8 + h], r2h.at[i, 1, h],
                   to_x).start()
        for h in (0, 1):
            arrived(g2.at[i, 4 + h, rows2, near2], r2.at[i, 3 + h])
            arrived(g2.at[i, 4 + h, rows2, far2], r2c.at[i, h])
        remote(g2.at[i, pl.ds(4, 3)], g2.at[i, pl.ds(12, 3)], s2.at[lax.rem(PIECES + i, RING), 10], r2s.at[i, 1], to_s).start()

    def third2(i):
        for h in (0, 1):
            arrived(g2.at[i, 7, rows2, half2[h]], r2h.at[i, 1, h])
        remote(g2.at[i, 7], g2.at[i, 15], s2.at[lax.rem(PIECES + i, RING), 11], r2s.at[i, 2], to_s).start()

    def from_sibling(i, groups):
        for group in groups:
            ref = g2.at[i, pl.ds(8, 4)] if group == 0 else g2.at[i, pl.ds(12, 3)] if group == 1 else g2.at[i, 15]
            arrived(ref, r2s.at[i, group])

    def drain2(i):
        for k in (0, 1, 2, 11):
            left(g2.at[i, 0], s2.at[lax.rem(PIECES + i, RING), k])
        for k in (3, 4):
            left(g2.at[i, 0, rows2, near2], s2.at[lax.rem(PIECES + i, RING), k])
        for k in (12, 13):
            left(g2.at[i, 0, rows2, far2], s2.at[lax.rem(PIECES + i, RING), k])
        for k in (5, 6, 8, 9):
            left(g2.at[i, 0, rows2, half2[0]], s2.at[lax.rem(PIECES + i, RING), k])
        left(g2.at[i, pl.ds(0, 4)], s2.at[lax.rem(PIECES + i, RING), 7])
        left(g2.at[i, pl.ds(4, 3)], s2.at[lax.rem(PIECES + i, RING), 10])

    def keep(q, slots, scores):
        for n, (p, k) in enumerate(slots):
            dx, dz = SLOTS[k]
            sx, sz = (1 - xh if dx else xh), lax.rem(z + dz, 4)
            row = pl.multiple_of(lax.rem(sz, 2) * 32 + (1 - c if p else c) * 16, 16)
            cs[lax.rem(q, 4), sx * 2 + sz // 2, pl.ds(row, 16), :] = scores[n * 16 : n * 16 + 16].astype(BF)

    every = [(p, k) for p in range(2) for k in range(8)]
    early = [(p, k) for p in range(2) for k in range(4)]
    late = [(p, k) for p in range(2) for k in range(4, 8)]

    def to_y(q):
        for d in (1, 2, 3):
            remote(cs.at[lax.rem(q, 4), lax.rem(y + d, 4)], yr.at[q, d - 1], ysend.at[lax.rem(q, 4), d - 1], ysem.at[q, d - 1],
                   to_lay[d, 0]).start()

    def over_y(q):
        total = cs[lax.rem(q, 4), y].astype(F32)
        for d in range(3):
            arrived(yr.at[q, d], ysem.at[q, d])
            left(yr.at[q, d], ysend.at[lax.rem(q, 4), d])
            total += yr[q, d].astype(F32)
        ysum[lax.rem(q, 4)] = total.reshape(2, 32, 512)
        xs[lax.rem(q, 4)] = ysum[lax.rem(q, 4), 1 - xl].astype(BF)
        remote(xs.at[lax.rem(q, 4)], xr.at[q], xsend.at[lax.rem(q, 4)], xsem.at[q], to_lay[0, 1]).start()

    def finish(q, total):
        for k in range(2):
            out[pl.ds(pl.multiple_of(k * 128 + q * 16, 16), 16), :] = total[k * 16 : k * 16 + 16]

    def over_x(q):
        arrived(xr.at[q], xsem.at[q])
        left(xr.at[q], xsend.at[lax.rem(q, 4)])
        finish(q, ysum[lax.rem(q, 4), xl] + xr[q].astype(F32))

    def main_head(q):
        rows = pl.ds(pl.multiple_of(q * 16, 16), 16)
        acc[1] = jnp.zeros((256, 512), F32)

        @pl.loop(0, PIECES // 2)
        def _(j):
            cols = pl.ds(pl.multiple_of(j * 1024, 1024), 1024)
            for l in (0, 1):
                lhs = g1[j * 2 + l, :, rows, :].reshape(256, 1024)
                acc[1] += lax.dot_general(lhs, bmat[l, :, cols], NT, preferred_element_type=F32)

        keep(q, every, acc[1])
        to_y(q)

    def product(l, lhs):
        return lax.dot_general(lhs, bmat[l], NT, preferred_element_type=F32)

    def main_item(n):
        l = lax.rem(n, 2)
        acc[0] = jnp.where(l == 0, jnp.zeros((256, 512), F32), acc[0]) + product(l, g2[n].reshape(256, 4096))

        @pl.when(l == 1)
        def _():
            q = HEAD // 16 + n // 2
            keep(q, every, acc[0])
            to_y(q)

    fetch(-1).wait()
    split_layers(0, write_a)
    fetch(1).start()
    prepare(0)
    pl.semaphore_wait(barrier, 11)

    end1, end2 = PIECES, PIECES + ITEMS

    @pl.loop(0, end2 + 3)
    def _(t):
        def during(start, stop, do, odd=None):
            on = (t >= start) & (t < stop)
            if odd is not None:
                on = on & (lax.rem(t, 2) == odd)
            pl.when(on)(do)

        def head_from_sibling():
            @pl.loop(0, PIECES)
            def _(p):
                for group in (0, 1):
                    arrived(g1.at[p, pl.ds(8 + 4 * group, 4)], r1s.at[p, group])

        during(RING, end1 + RING, lambda: drain1(t - RING))
        during(end1 + RING, end2 + RING, lambda: drain2(t - end1 - RING))
        during(0, end1, lambda: own1(t))
        during(end1, end2, lambda: own2(t - end1))
        during(1, end1 + 1, lambda: first1(t - 1))
        during(end1 + 1, end2 + 1, lambda: first2(t - end1 - 1))
        during(2, end1 + 2, lambda: second1(t - 2))
        during(end1 + 2, end2 + 2, lambda: second2(t - end1 - 2))

        def item():
            from_sibling(t - end1 - 4, (0, 1, 2))
            main_item(t - end1 - 4)

        first_main = end1 + 3
        heads = HEAD // 16
        during(first_main, first_main + 1, head_from_sibling)
        during(first_main, first_main + heads, lambda: main_head(t - first_main))
        during(end1 + 4, end2 + 3, item)
        during(first_main + 1, first_main + 1 + heads, lambda: over_y(t - first_main - 1))
        during(end1 + 6, end2 + 3, lambda: over_y(heads + (t - end1 - 6) // 2), end1 % 2)
        during(first_main + 2, first_main + 2 + heads, lambda: over_x(t - first_main - 2))
        during(end1 + 7, end2 + 3, lambda: over_x(heads + (t - end1 - 7) // 2), 1 - end1 % 2)
        during(3, end1 + 3, lambda: third1(t - 3))
        during(0, end1 - 1, lambda: prepare(t + 1))
        during(end1 - 1, end1 + 3, lambda: split_train(t - end1 + 1))
        during(end1 + 3, end2 + 2, lambda: third2(t - end1 - 3))

    i, q = ITEMS - 1, QUEUE - 1

    def last(k, slots):
        lhs = jnp.concatenate([g2[i, p + k : p + k + 4].reshape(64, 4096) for p in (0, 8)], axis=0)
        done = jnp.concatenate([acc[0, (p + k) * 16 : (p + k) * 16 + 64] for p in (0, 8)], axis=0)
        keep(q, slots, done + product(1, lhs))

    from_sibling(i, (0,))
    last(0, early)
    third2(i)

    from_sibling(i, (1, 2))
    last(4, late)
    mine = pl.ds(pl.multiple_of(xl * 32, 32), 32)
    yours = pl.ds(pl.multiple_of(32 - xl * 32, 32), 32)
    for n, (d, f) in enumerate(others):
        remote(cs.at[q % 4, lax.rem(y + d, 4), yours if f else mine], zr.at[n], zsend.at[n], zsem.at[n],
               to_lay[d, f]).start()
    for n in range(end2 + 3 - RING, end2):
        drain2(n - end1)
    total = cs[q % 4, y, mine, :].astype(F32)
    for n in range(len(others)):
        arrived(zr.at[n], zsem.at[n])
        total += zr[n].astype(F32)
    finish(q, total)
    over_x(q - 1)
    for n in range(len(others)):
        left(zr.at[n], zsend.at[n])


def body(train, test, inv_out, inv_in):
    vmem, hbm = pl.BlockSpec(memory_space=pltpu.VMEM), pl.BlockSpec(memory_space=pl.ANY)
    dma = pltpu.SemaphoreType.DMA
    return pl.pallas_call(
        kernel,
        out_shape=jax.ShapeDtypeStruct((256, 512), F32),
        in_specs=[hbm, hbm, vmem, vmem],
        out_specs=vmem,
        scratch_shapes=[
            pltpu.VMEM((PIECES, 16, HEAD, 1024), BF),
            pltpu.VMEM((ITEMS, 16, ROWS, 4096), BF),
            pltpu.VMEM((2, 512, 4096), BF),
            pltpu.VMEM((2, 256, 4096), BF),
            pltpu.VMEM((2, 128, 4096), BF),
            pltpu.VMEM((4096, PART), BF),
            pltpu.VMEM((4, 4, 64, 512), BF),
            pltpu.VMEM((QUEUE - 1, 3, 64, 512), BF),
            pltpu.VMEM((4, 32, 512), BF),
            pltpu.VMEM((QUEUE - 1, 32, 512), BF),
            pltpu.VMEM((4, 2, 32, 512), F32),
            pltpu.VMEM((7, 32, 512), BF),
            pltpu.VMEM((2, 256, 512), F32),
            dma((PIECES, 5)),
            dma((PIECES, 2, 2)),
            dma((PIECES, 2)),
            dma((PIECES, 2)),
            dma((ITEMS, 5)),
            dma((ITEMS, 2, 2)),
            dma((ITEMS, 2)),
            dma((ITEMS, 3)),
            dma((RING, 14)),
            dma((QUEUE - 1, 3)),
            dma((4, 3)),
            dma((QUEUE - 1,)),
            dma((4,)),
            dma((7,)),
            dma((7,)),
            dma((2,)),
        ],
        compiler_params=pltpu.CompilerParams(
            collective_id=0, has_side_effects=True, vmem_limit_bytes=62 * 2**20
        ),
        cost_estimate=pl.CostEstimate(flops=26 * 10**9, bytes_accessed=12 * 2**20, transcendentals=0),
    )(train, test, inv_out, inv_in)


def solution(mesh):
    return jax.shard_map(
        body,
        mesh=mesh,
        in_specs=(P("ex", "lay", None), P("ex", "lay", None), P("lay", None, None), P("lay", None, None)),
        out_specs=P("lay", "ex"),
        check_vma=False,
    )
```

```python
import jax
import jax.numpy as jnp
from jax import lax
from jax.experimental import pallas as pl
from jax.experimental.pallas import tpu as pltpu
from jax.sharding import PartitionSpec as P

BF, F32 = jnp.bfloat16, jnp.float32
NT = (((1,), (1,)), ((), ()))
TN = (((0,), (0,)), ((), ()))
HIGHEST = lax.Precision.HIGHEST

SLOTS = ((0, 0), (1, 0), (0, 3), (0, 1), (1, 3), (1, 1), (0, 2), (1, 2))
PIECES = 8
HEAD = 64
ROWS = 16
ITEMS = 8
QUEUE = 8
PART = 512
CUT1, CUT2 = 896, 3584
RING = 5


def iota(shape, dim):
    return lax.broadcasted_iota(jnp.int32, shape, dim)


def kernel(train, test, inv_out, inv_in, out, g1, g2, bmat, stage, amat, weight, cs, yr, xs, xr, ysum, zr, acc,
           r1, r1h, r1c, r1s, r2, r2h, r2c, r2s, s2, ysem, ysend, xsem, xsend, zsem, zsend, local):
    ex, lay = lax.axis_index("ex"), lax.axis_index("lay")
    xh, z, c = ex // 8, (ex // 2) % 4, ex % 2
    y, xl = lay // 2, lay % 2

    def at(xh_, z_, c_):
        return (xh_ * 8 + z_ * 2 + c_, lay)

    to_x, to_s = at(1 - xh, z, c), at(xh, z, 1 - c)
    to_up, to_down = at(xh, lax.rem(z + 1, 4), c), at(xh, lax.rem(z + 3, 4), c)
    others = [(d, f) for f in (0, 1) for d in range(4) if d or f]
    to_lay = {(d, f): (ex, lax.rem(y + d, 4) * 2 + (1 - xl if f else xl)) for d, f in others}

    def remote(src, dst, send, recv, device):
        return pltpu.make_async_remote_copy(src_ref=src, dst_ref=dst, send_sem=send, recv_sem=recv,
                                            device_id=device, device_id_type=pl.DeviceIdType.MESH)

    def arrived(ref, recv):
        remote(ref, ref, s2.at[0, 0], recv, to_x).wait_recv()

    def left(ref, send):
        remote(ref, ref, send, r1.at[0, 0], to_x).wait_send()

    def fetch(i):
        if i < 0:
            src = test.reshape(256, 4096)
        else:
            src = train.reshape(1024, 4096).at[pl.ds(i * 256, 256)]
        return pltpu.make_async_copy(src, stage.at[(i + 1) % 2], local.at[(i + 1) % 2])

    fetch(-1).start()
    fetch(0).start()
    barrier = pltpu.get_barrier_semaphore()
    for device in [to_x, to_up, to_down, to_s] + [to_lay[k] for k in others]:
        pl.semaphore_signal(barrier, inc=1, device_id=device, device_id_type=pl.DeviceIdType.MESH)

    def weigh(l, j):
        r, col = iota((64, PART), 0), iota((64, PART), 1)
        e = lax.dot_general(inv_out[l], (r == (PART // 64) * j + col // 64).astype(F32), TN,
                            precision=HIGHEST, preferred_element_type=F32)
        f = jnp.dot(inv_in[l], (r == col % 64).astype(F32), precision=HIGHEST, preferred_element_type=F32)
        weight[...] = (e[:, None, :] * f[None]).astype(BF).reshape(4096, PART)

    def precondition(l, quarter, part):
        j = quarter * 2 + part
        value = jnp.dot(amat[l], weight[...], preferred_element_type=F32).astype(BF)
        g1[quarter * 2 + l, 0, :, pl.ds(pl.multiple_of(part * PART, PART), PART)] = value[:HEAD]
        cols = pl.ds(pl.multiple_of(j * PART, PART), PART)
        for i in range(ITEMS // 2):
            g2[i * 2 + l, 0, :, cols] = value[HEAD + i * ROWS : HEAD + (i + 1) * ROWS]

    def split_layers(slot, write):
        ri, ci = iota((256, 256), 0), iota((256, 256), 1)
        order = (ci == 2 * (ri % 128) + ri // 128).astype(BF)

        @pl.loop(0, 8)
        def _(i):
            cols = pl.ds(pl.multiple_of(i * 512, 512), 512)
            write(cols, jnp.dot(order, stage[slot, :, cols], preferred_element_type=F32).astype(BF))

    def write_a(cols, value):
        amat[0, :, cols] = value[:128]
        amat[1, :, cols] = value[128:]

    def split_train(t):
        slot = lax.rem(t + 1, 2)

        def write_b(cols, value):
            rows = pl.ds(pl.multiple_of(t * 128, 128), 128)
            bmat[0, rows, cols] = value[:128]
            bmat[1, rows, cols] = value[128:]

        pltpu.make_async_copy(train.reshape(1024, 4096).at[pl.ds(0, 256)], stage.at[slot], local.at[slot]).wait()
        split_layers(slot, write_b)

        @pl.when(t < 2)
        def _():
            start = pl.multiple_of((t + 2) * 256, 256)
            pltpu.make_async_copy(train.reshape(1024, 4096).at[pl.ds(start, 256)], stage.at[slot],
                                  local.at[slot]).start()

    def prepare(p):
        l, quarter = lax.rem(p, 2), p // 2

        @pl.loop(0, 2)
        def _(part):
            weigh(l, quarter * 2 + part)
            precondition(l, quarter, part)

    half1 = [pl.ds(h * HEAD // 2, HEAD // 2) for h in (0, 1)]
    rows1, near1, far1 = pl.ds(0, HEAD), pl.ds(0, CUT1), pl.ds(CUT1, 1024 - CUT1)

    def own1(p):
        ref = g1.at[p, 0]
        remote(ref, g1.at[p, 2], s2.at[lax.rem(p, RING), 1], r1.at[p, 1], to_up).start()
        remote(ref, g1.at[p, 3], s2.at[lax.rem(p, RING), 2], r1.at[p, 2], to_down).start()
        remote(ref, g1.at[p, 1], s2.at[lax.rem(p, RING), 0], r1.at[p, 0], to_x).start()

    def first1(p):
        for h, device in ((0, to_up), (1, to_down)):
            arrived(g1.at[p, 2 + h], r1.at[p, 1 + h])
            remote(g1.at[p, 2 + h, half1[h]], g1.at[p, 6, half1[h]], s2.at[lax.rem(p, RING), 5 + h], r1h.at[p, 0, h], device).start()
            remote(g1.at[p, 2 + h, rows1, far1], g1.at[p, 4 + h, rows1, far1], s2.at[lax.rem(p, RING), 11 + h], r1c.at[p, h],
                   to_x).start()
        arrived(g1.at[p, 1], r1.at[p, 0])
        for h, device in ((0, to_up), (1, to_down)):
            remote(g1.at[p, 1, rows1, near1], g1.at[p, 4 + h, rows1, near1], s2.at[lax.rem(p, RING), 3 + h], r1.at[p, 3 + h],
                   device).start()
        remote(g1.at[p, pl.ds(0, 4)], g1.at[p, pl.ds(8, 4)], s2.at[lax.rem(p, RING), 7], r1s.at[p, 0], to_s).start()

    def second1(p):
        for h in (0, 1):
            arrived(g1.at[p, 6, half1[h]], r1h.at[p, 0, h])
            remote(g1.at[p, 6, half1[h]], g1.at[p, 7, half1[h]], s2.at[lax.rem(p, RING), 8 + h], r1h.at[p, 1, h], to_x).start()
        for h in (0, 1):
            arrived(g1.at[p, 4 + h, rows1, near1], r1.at[p, 3 + h])
            arrived(g1.at[p, 4 + h, rows1, far1], r1c.at[p, h])

    def third1(p):
        for h in (0, 1):
            arrived(g1.at[p, 7, half1[h]], r1h.at[p, 1, h])
        remote(g1.at[p, pl.ds(4, 4)], g1.at[p, pl.ds(12, 4)], s2.at[lax.rem(p, RING), 10], r1s.at[p, 1], to_s).start()

    def drain1(p):
        for k in (0, 1, 2):
            left(g1.at[p, 0], s2.at[lax.rem(p, RING), k])
        for k in (3, 4):
            left(g1.at[p, 0, rows1, near1], s2.at[lax.rem(p, RING), k])
        for k in (11, 12):
            left(g1.at[p, 0, rows1, far1], s2.at[lax.rem(p, RING), k])
        for k in (5, 6, 8, 9):
            left(g1.at[p, 0, half1[0]], s2.at[lax.rem(p, RING), k])
        for k, group in ((7, 0), (10, 1)):
            left(g1.at[p, pl.ds(0, 4)], s2.at[lax.rem(p, RING), k])

    half2 = [pl.ds(h * 2048, 2048) for h in (0, 1)]
    rows2, near2, far2 = pl.ds(0, ROWS), pl.ds(0, CUT2), pl.ds(CUT2, 4096 - CUT2)

    def own2(i):
        ref = g2.at[i, 0]
        remote(ref, g2.at[i, 2], s2.at[lax.rem(PIECES + i, RING), 1], r2.at[i, 1], to_up).start()
        remote(ref, g2.at[i, 3], s2.at[lax.rem(PIECES + i, RING), 2], r2.at[i, 2], to_down).start()
        remote(ref, g2.at[i, 1], s2.at[lax.rem(PIECES + i, RING), 0], r2.at[i, 0], to_x).start()

    def first2(i):
        for h, device in ((0, to_up), (1, to_down)):
            arrived(g2.at[i, 2 + h], r2.at[i, 1 + h])
            remote(g2.at[i, 2 + h, rows2, half2[h]], g2.at[i, 6, rows2, half2[h]], s2.at[lax.rem(PIECES + i, RING), 5 + h], r2h.at[i, 0, h],
                   device).start()
            remote(g2.at[i, 2 + h, rows2, far2], g2.at[i, 4 + h, rows2, far2], s2.at[lax.rem(PIECES + i, RING), 12 + h], r2c.at[i, h],
                   to_x).start()
        arrived(g2.at[i, 1], r2.at[i, 0])
        for h, device in ((0, to_up), (1, to_down)):
            remote(g2.at[i, 1, rows2, near2], g2.at[i, 4 + h, rows2, near2], s2.at[lax.rem(PIECES + i, RING), 3 + h], r2.at[i, 3 + h],
                   device).start()
        remote(g2.at[i, pl.ds(0, 4)], g2.at[i, pl.ds(8, 4)], s2.at[lax.rem(PIECES + i, RING), 7], r2s.at[i, 0], to_s).start()

    def second2(i):
        for h in (0, 1):
            arrived(g2.at[i, 6, rows2, half2[h]], r2h.at[i, 0, h])
            remote(g2.at[i, 6, rows2, half2[h]], g2.at[i, 7, rows2, half2[h]], s2.at[lax.rem(PIECES + i, RING), 8 + h], r2h.at[i, 1, h],
                   to_x).start()
        for h in (0, 1):
            arrived(g2.at[i, 4 + h, rows2, near2], r2.at[i, 3 + h])
            arrived(g2.at[i, 4 + h, rows2, far2], r2c.at[i, h])
        remote(g2.at[i, pl.ds(4, 3)], g2.at[i, pl.ds(12, 3)], s2.at[lax.rem(PIECES + i, RING), 10], r2s.at[i, 1], to_s).start()

    def third2(i):
        for h in (0, 1):
            arrived(g2.at[i, 7, rows2, half2[h]], r2h.at[i, 1, h])
        remote(g2.at[i, 7], g2.at[i, 15], s2.at[lax.rem(PIECES + i, RING), 11], r2s.at[i, 2], to_s).start()

    def from_sibling(i, groups):
        for group in groups:
            ref = g2.at[i, pl.ds(8, 4)] if group == 0 else g2.at[i, pl.ds(12, 3)] if group == 1 else g2.at[i, 15]
            arrived(ref, r2s.at[i, group])

    def drain2(i):
        for k in (0, 1, 2, 11):
            left(g2.at[i, 0], s2.at[lax.rem(PIECES + i, RING), k])
        for k in (3, 4):
            left(g2.at[i, 0, rows2, near2], s2.at[lax.rem(PIECES + i, RING), k])
        for k in (12, 13):
            left(g2.at[i, 0, rows2, far2], s2.at[lax.rem(PIECES + i, RING), k])
        for k in (5, 6, 8, 9):
            left(g2.at[i, 0, rows2, half2[0]], s2.at[lax.rem(PIECES + i, RING), k])
        left(g2.at[i, pl.ds(0, 4)], s2.at[lax.rem(PIECES + i, RING), 7])
        left(g2.at[i, pl.ds(4, 3)], s2.at[lax.rem(PIECES + i, RING), 10])

    def keep(q, slots, scores):
        for n, (p, k) in enumerate(slots):
            dx, dz = SLOTS[k]
            sx, sz = (1 - xh if dx else xh), lax.rem(z + dz, 4)
            row = pl.multiple_of(lax.rem(sz, 2) * 32 + (1 - c if p else c) * 16, 16)
            cs[lax.rem(q, 4), sx * 2 + sz // 2, pl.ds(row, 16), :] = scores[n * 16 : n * 16 + 16].astype(BF)

    every = [(p, k) for p in range(2) for k in range(8)]
    early = [(p, k) for p in range(2) for k in range(4)]
    late = [(p, k) for p in range(2) for k in range(4, 8)]

    def to_y(q):
        for d in (1, 2, 3):
            remote(cs.at[lax.rem(q, 4), lax.rem(y + d, 4)], yr.at[q, d - 1], ysend.at[lax.rem(q, 4), d - 1], ysem.at[q, d - 1],
                   to_lay[d, 0]).start()

    def over_y(q):
        total = cs[lax.rem(q, 4), y].astype(F32)
        for d in range(3):
            arrived(yr.at[q, d], ysem.at[q, d])
            left(yr.at[q, d], ysend.at[lax.rem(q, 4), d])
            total += yr[q, d].astype(F32)
        ysum[lax.rem(q, 4)] = total.reshape(2, 32, 512)
        xs[lax.rem(q, 4)] = ysum[lax.rem(q, 4), 1 - xl].astype(BF)
        remote(xs.at[lax.rem(q, 4)], xr.at[q], xsend.at[lax.rem(q, 4)], xsem.at[q], to_lay[0, 1]).start()

    def finish(q, total):
        for k in range(2):
            out[pl.ds(pl.multiple_of(k * 128 + q * 16, 16), 16), :] = total[k * 16 : k * 16 + 16]

    def over_x(q):
        arrived(xr.at[q], xsem.at[q])
        left(xr.at[q], xsend.at[lax.rem(q, 4)])
        finish(q, ysum[lax.rem(q, 4), xl] + xr[q].astype(F32))

    def main_head(q):
        rows = pl.ds(pl.multiple_of(q * 16, 16), 16)
        acc[1] = jnp.zeros((256, 512), F32)

        @pl.loop(0, PIECES // 2)
        def _(j):
            cols = pl.ds(pl.multiple_of(j * 1024, 1024), 1024)
            for l in (0, 1):
                lhs = g1[j * 2 + l, :, rows, :].reshape(256, 1024)
                acc[1] += lax.dot_general(lhs, bmat[l, :, cols], NT, preferred_element_type=F32)

        keep(q, every, acc[1])
        to_y(q)

    def product(l, lhs):
        return lax.dot_general(lhs, bmat[l], NT, preferred_element_type=F32)

    def main_item(n):
        l = lax.rem(n, 2)
        acc[0] = jnp.where(l == 0, jnp.zeros((256, 512), F32), acc[0]) + product(l, g2[n].reshape(256, 4096))

        @pl.when(l == 1)
        def _():
            q = HEAD // 16 + n // 2
            keep(q, every, acc[0])
            to_y(q)

    fetch(-1).wait()
    split_layers(0, write_a)
    fetch(1).start()
    prepare(0)
    pl.semaphore_wait(barrier, 11)

    end1, end2 = PIECES, PIECES + ITEMS

    @pl.loop(0, end2 + 3)
    def _(t):
        def during(start, stop, do, odd=None):
            on = (t >= start) & (t < stop)
            if odd is not None:
                on = on & (lax.rem(t, 2) == odd)
            pl.when(on)(do)

        def head_from_sibling():
            @pl.loop(0, PIECES)
            def _(p):
                for group in (0, 1):
                    arrived(g1.at[p, pl.ds(8 + 4 * group, 4)], r1s.at[p, group])

        during(RING, end1 + RING, lambda: drain1(t - RING))
        during(end1 + RING, end2 + RING, lambda: drain2(t - end1 - RING))
        during(0, end1, lambda: own1(t))
        during(end1, end2, lambda: own2(t - end1))
        during(1, end1 + 1, lambda: first1(t - 1))
        during(end1 + 1, end2 + 1, lambda: first2(t - end1 - 1))
        during(2, end1 + 2, lambda: second1(t - 2))
        during(end1 + 2, end2 + 2, lambda: second2(t - end1 - 2))

        def item():
            from_sibling(t - end1 - 4, (0, 1, 2))
            main_item(t - end1 - 4)

        first_main = end1 + 3
        heads = HEAD // 16
        during(first_main, first_main + 1, head_from_sibling)
        during(first_main, first_main + heads, lambda: main_head(t - first_main))
        during(end1 + 4, end2 + 3, item)
        during(first_main + 1, first_main + 1 + heads, lambda: over_y(t - first_main - 1))
        during(end1 + 6, end2 + 3, lambda: over_y(heads + (t - end1 - 6) // 2), end1 % 2)
        during(first_main + 2, first_main + 2 + heads, lambda: over_x(t - first_main - 2))
        during(end1 + 7, end2 + 3, lambda: over_x(heads + (t - end1 - 7) // 2), 1 - end1 % 2)
        during(3, end1 + 3, lambda: third1(t - 3))
        during(0, end1 - 1, lambda: prepare(t + 1))
        during(end1 - 1, end1 + 3, lambda: split_train(t - end1 + 1))
        during(end1 + 3, end2 + 2, lambda: third2(t - end1 - 3))

    i, q = ITEMS - 1, QUEUE - 1

    def last(k, slots):
        lhs = jnp.concatenate([g2[i, p + k : p + k + 4].reshape(64, 4096) for p in (0, 8)], axis=0)
        done = jnp.concatenate([acc[0, (p + k) * 16 : (p + k) * 16 + 64] for p in (0, 8)], axis=0)
        keep(q, slots, done + product(1, lhs))

    third2(i)
    from_sibling(i, (0,))
    last(0, early)

    from_sibling(i, (1, 2))
    last(4, late)
    mine = pl.ds(pl.multiple_of(xl * 32, 32), 32)
    yours = pl.ds(pl.multiple_of(32 - xl * 32, 32), 32)
    for n, (d, f) in enumerate(others):
        remote(cs.at[q % 4, lax.rem(y + d, 4), yours if f else mine], zr.at[n], zsend.at[n], zsem.at[n],
               to_lay[d, f]).start()
    for n in range(end2 + 3 - RING, end2):
        drain2(n - end1)
    total = cs[q % 4, y, mine, :].astype(F32)
    for n in range(len(others)):
        arrived(zr.at[n], zsem.at[n])
        total += zr[n].astype(F32)
    finish(q, total)
    over_x(q - 1)
    for n in range(len(others)):
        left(zr.at[n], zsend.at[n])


def body(train, test, inv_out, inv_in):
    vmem, hbm = pl.BlockSpec(memory_space=pltpu.VMEM), pl.BlockSpec(memory_space=pl.ANY)
    dma = pltpu.SemaphoreType.DMA
    return pl.pallas_call(
        kernel,
        out_shape=jax.ShapeDtypeStruct((256, 512), F32),
        in_specs=[hbm, hbm, vmem, vmem],
        out_specs=vmem,
        scratch_shapes=[
            pltpu.VMEM((PIECES, 16, HEAD, 1024), BF),
            pltpu.VMEM((ITEMS, 16, ROWS, 4096), BF),
            pltpu.VMEM((2, 512, 4096), BF),
            pltpu.VMEM((2, 256, 4096), BF),
            pltpu.VMEM((2, 128, 4096), BF),
            pltpu.VMEM((4096, PART), BF),
            pltpu.VMEM((4, 4, 64, 512), BF),
            pltpu.VMEM((QUEUE - 1, 3, 64, 512), BF),
            pltpu.VMEM((4, 32, 512), BF),
            pltpu.VMEM((QUEUE - 1, 32, 512), BF),
            pltpu.VMEM((4, 2, 32, 512), F32),
            pltpu.VMEM((7, 32, 512), BF),
            pltpu.VMEM((2, 256, 512), F32),
            dma((PIECES, 5)),
            dma((PIECES, 2, 2)),
            dma((PIECES, 2)),
            dma((PIECES, 2)),
            dma((ITEMS, 5)),
            dma((ITEMS, 2, 2)),
            dma((ITEMS, 2)),
            dma((ITEMS, 3)),
            dma((RING, 14)),
            dma((QUEUE - 1, 3)),
            dma((4, 3)),
            dma((QUEUE - 1,)),
            dma((4,)),
            dma((7,)),
            dma((7,)),
            dma((2,)),
        ],
        compiler_params=pltpu.CompilerParams(
            collective_id=0, has_side_effects=True, vmem_limit_bytes=62 * 2**20
        ),
        cost_estimate=pl.CostEstimate(flops=26 * 10**9, bytes_accessed=12 * 2**20, transcendentals=0),
    )(train, test, inv_out, inv_in)


def solution(mesh):
    return jax.shard_map(
        body,
        mesh=mesh,
        in_specs=(P("ex", "lay", None), P("ex", "lay", None), P("lay", None, None), P("lay", None, None)),
        out_specs=P("lay", "ex"),
        check_vma=False,
    )
```

```python
import jax
import jax.numpy as jnp
from jax import lax
from jax.experimental import pallas as pl
from jax.experimental.pallas import tpu as pltpu
from jax.sharding import PartitionSpec as P

BF, F32 = jnp.bfloat16, jnp.float32
NT = (((1,), (1,)), ((), ()))
TN = (((0,), (0,)), ((), ()))
HIGHEST = lax.Precision.HIGHEST

SLOTS = ((0, 0), (1, 0), (0, 3), (0, 1), (1, 3), (1, 1), (0, 2), (1, 2))
PIECES = 8
HEAD = 64
ROWS = 16
ITEMS = 8
QUEUE = 8
PART = 512
CUT1, CUT2 = 896, 3840
RING = 5


def iota(shape, dim):
    return lax.broadcasted_iota(jnp.int32, shape, dim)


def kernel(train, test, inv_out, inv_in, result, out, osem, g1, g2, bmat, stage, amat, weight, cs, yr, xs, xr, ysum, zr, acc,
           r1, r1h, r1c, r1s, r2, r2h, r2c, r2s, s2, ysem, ysend, xsem, xsend, zsem, zsend, local):
    ex, lay = lax.axis_index("ex"), lax.axis_index("lay")
    xh, z, c = ex // 8, (ex // 2) % 4, ex % 2
    y, xl = lay // 2, lay % 2

    def at(xh_, z_, c_):
        return (xh_ * 8 + z_ * 2 + c_, lay)

    to_x, to_s = at(1 - xh, z, c), at(xh, z, 1 - c)
    to_up, to_down = at(xh, lax.rem(z + 1, 4), c), at(xh, lax.rem(z + 3, 4), c)
    others = [(d, f) for f in (0, 1) for d in range(4) if d or f]
    to_lay = {(d, f): (ex, lax.rem(y + d, 4) * 2 + (1 - xl if f else xl)) for d, f in others}

    def remote(src, dst, send, recv, device):
        return pltpu.make_async_remote_copy(src_ref=src, dst_ref=dst, send_sem=send, recv_sem=recv,
                                            device_id=device, device_id_type=pl.DeviceIdType.MESH)

    def arrived(ref, recv):
        remote(ref, ref, s2.at[0, 0], recv, to_x).wait_recv()

    def left(ref, send):
        remote(ref, ref, send, r1.at[0, 0], to_x).wait_send()

    def fetch(i):
        if i < 0:
            src = test.reshape(256, 4096)
        else:
            src = train.reshape(1024, 4096).at[pl.ds(i * 256, 256)]
        return pltpu.make_async_copy(src, stage.at[(i + 1) % 2], local.at[(i + 1) % 2])

    fetch(-1).start()
    fetch(0).start()
    barrier = pltpu.get_barrier_semaphore()
    for device in [to_x, to_up, to_down, to_s] + [to_lay[k] for k in others]:
        pl.semaphore_signal(barrier, inc=1, device_id=device, device_id_type=pl.DeviceIdType.MESH)

    def weigh(l, j):
        r, col = iota((64, PART), 0), iota((64, PART), 1)
        e = lax.dot_general(inv_out[l], (r == (PART // 64) * j + col // 64).astype(F32), TN,
                            precision=HIGHEST, preferred_element_type=F32)
        f = jnp.dot(inv_in[l], (r == col % 64).astype(F32), precision=HIGHEST, preferred_element_type=F32)
        weight[...] = (e[:, None, :] * f[None]).astype(BF).reshape(4096, PART)

    def precondition(l, quarter, part):
        j = quarter * 2 + part
        value = jnp.dot(amat[l], weight[...], preferred_element_type=F32).astype(BF)
        g1[quarter * 2 + l, 0, :, pl.ds(pl.multiple_of(part * PART, PART), PART)] = value[:HEAD]
        cols = pl.ds(pl.multiple_of(j * PART, PART), PART)
        for i in range(ITEMS // 2):
            g2[i * 2 + l, 0, :, cols] = value[HEAD + i * ROWS : HEAD + (i + 1) * ROWS]

    def split_layers(slot, write):
        ri, ci = iota((256, 256), 0), iota((256, 256), 1)
        order = (ci == 2 * (ri % 128) + ri // 128).astype(BF)

        @pl.loop(0, 8)
        def _(i):
            cols = pl.ds(pl.multiple_of(i * 512, 512), 512)
            write(cols, jnp.dot(order, stage[slot, :, cols], preferred_element_type=F32).astype(BF))

    def write_a(cols, value):
        amat[0, :, cols] = value[:128]
        amat[1, :, cols] = value[128:]

    def split_train(t):
        slot = lax.rem(t + 1, 2)

        def write_b(cols, value):
            rows = pl.ds(pl.multiple_of(t * 128, 128), 128)
            bmat[0, rows, cols] = value[:128]
            bmat[1, rows, cols] = value[128:]

        pltpu.make_async_copy(train.reshape(1024, 4096).at[pl.ds(0, 256)], stage.at[slot], local.at[slot]).wait()
        split_layers(slot, write_b)

        @pl.when(t < 2)
        def _():
            start = pl.multiple_of((t + 2) * 256, 256)
            pltpu.make_async_copy(train.reshape(1024, 4096).at[pl.ds(start, 256)], stage.at[slot],
                                  local.at[slot]).start()

    def prepare(p):
        l, quarter = lax.rem(p, 2), p // 2

        @pl.loop(0, 2)
        def _(part):
            weigh(l, quarter * 2 + part)
            precondition(l, quarter, part)

    half1 = [pl.ds(h * HEAD // 2, HEAD // 2) for h in (0, 1)]
    rows1, near1, far1 = pl.ds(0, HEAD), pl.ds(0, CUT1), pl.ds(CUT1, 1024 - CUT1)

    def own1(p):
        ref = g1.at[p, 0]
        remote(ref, g1.at[p, 1], s2.at[lax.rem(p, RING), 0], r1.at[p, 0], to_x).start()
        remote(ref, g1.at[p, 2], s2.at[lax.rem(p, RING), 1], r1.at[p, 1], to_up).start()
        remote(ref, g1.at[p, 3], s2.at[lax.rem(p, RING), 2], r1.at[p, 2], to_down).start()

    def first1(p):
        for h, device in ((0, to_up), (1, to_down)):
            arrived(g1.at[p, 2 + h], r1.at[p, 1 + h])
            remote(g1.at[p, 2 + h, half1[h]], g1.at[p, 6, half1[h]], s2.at[lax.rem(p, RING), 5 + h], r1h.at[p, 0, h], device).start()
            remote(g1.at[p, 2 + h, rows1, far1], g1.at[p, 4 + h, rows1, far1], s2.at[lax.rem(p, RING), 11 + h], r1c.at[p, h],
                   to_x).start()
        arrived(g1.at[p, 1], r1.at[p, 0])
        for h, device in ((0, to_up), (1, to_down)):
            remote(g1.at[p, 1, rows1, near1], g1.at[p, 4 + h, rows1, near1], s2.at[lax.rem(p, RING), 3 + h], r1.at[p, 3 + h],
                   device).start()
        remote(g1.at[p, pl.ds(0, 4)], g1.at[p, pl.ds(8, 4)], s2.at[lax.rem(p, RING), 7], r1s.at[p, 0], to_s).start()

    def second1(p):
        for h in (0, 1):
            arrived(g1.at[p, 6, half1[h]], r1h.at[p, 0, h])
            remote(g1.at[p, 6, half1[h]], g1.at[p, 7, half1[h]], s2.at[lax.rem(p, RING), 8 + h], r1h.at[p, 1, h], to_x).start()
        for h in (0, 1):
            arrived(g1.at[p, 4 + h, rows1, near1], r1.at[p, 3 + h])
            arrived(g1.at[p, 4 + h, rows1, far1], r1c.at[p, h])

    def third1(p):
        for h in (0, 1):
            arrived(g1.at[p, 7, half1[h]], r1h.at[p, 1, h])
        remote(g1.at[p, pl.ds(4, 4)], g1.at[p, pl.ds(12, 4)], s2.at[lax.rem(p, RING), 10], r1s.at[p, 1], to_s).start()

    def drain1(p):
        for k in (0, 1, 2):
            left(g1.at[p, 0], s2.at[lax.rem(p, RING), k])
        for k in (3, 4):
            left(g1.at[p, 0, rows1, near1], s2.at[lax.rem(p, RING), k])
        for k in (11, 12):
            left(g1.at[p, 0, rows1, far1], s2.at[lax.rem(p, RING), k])
        for k in (5, 6, 8, 9):
            left(g1.at[p, 0, half1[0]], s2.at[lax.rem(p, RING), k])
        for k, group in ((7, 0), (10, 1)):
            left(g1.at[p, pl.ds(0, 4)], s2.at[lax.rem(p, RING), k])

    half2 = [pl.ds(h * 2048, 2048) for h in (0, 1)]
    rows2, near2, far2 = pl.ds(0, ROWS), pl.ds(0, CUT2), pl.ds(CUT2, 4096 - CUT2)

    def own2(i):
        ref = g2.at[i, 0]
        remote(ref, g2.at[i, 1], s2.at[lax.rem(PIECES + i, RING), 0], r2.at[i, 0], to_x).start()
        remote(ref, g2.at[i, 2], s2.at[lax.rem(PIECES + i, RING), 1], r2.at[i, 1], to_up).start()
        remote(ref, g2.at[i, 3], s2.at[lax.rem(PIECES + i, RING), 2], r2.at[i, 2], to_down).start()

    def first2(i):
        for h, device in ((0, to_up), (1, to_down)):
            arrived(g2.at[i, 2 + h], r2.at[i, 1 + h])
            remote(g2.at[i, 2 + h, rows2, half2[h]], g2.at[i, 6, rows2, half2[h]], s2.at[lax.rem(PIECES + i, RING), 5 + h], r2h.at[i, 0, h],
                   device).start()
            remote(g2.at[i, 2 + h, rows2, far2], g2.at[i, 4 + h, rows2, far2], s2.at[lax.rem(PIECES + i, RING), 12 + h], r2c.at[i, h],
                   to_x).start()
        arrived(g2.at[i, 1], r2.at[i, 0])
        for h, device in ((0, to_up), (1, to_down)):
            remote(g2.at[i, 1, rows2, near2], g2.at[i, 4 + h, rows2, near2], s2.at[lax.rem(PIECES + i, RING), 3 + h], r2.at[i, 3 + h],
                   device).start()
        remote(g2.at[i, pl.ds(0, 4)], g2.at[i, pl.ds(8, 4)], s2.at[lax.rem(PIECES + i, RING), 7], r2s.at[i, 0], to_s).start()

    def second2(i):
        for h in (0, 1):
            arrived(g2.at[i, 6, rows2, half2[h]], r2h.at[i, 0, h])
            remote(g2.at[i, 6, rows2, half2[h]], g2.at[i, 7, rows2, half2[h]], s2.at[lax.rem(PIECES + i, RING), 8 + h], r2h.at[i, 1, h],
                   to_x).start()
        for h in (0, 1):
            arrived(g2.at[i, 4 + h, rows2, near2], r2.at[i, 3 + h])
            arrived(g2.at[i, 4 + h, rows2, far2], r2c.at[i, h])
        remote(g2.at[i, pl.ds(4, 3)], g2.at[i, pl.ds(12, 3)], s2.at[lax.rem(PIECES + i, RING), 10], r2s.at[i, 1], to_s).start()

    def third2(i):
        for h in (0, 1):
            arrived(g2.at[i, 7, rows2, half2[h]], r2h.at[i, 1, h])
        remote(g2.at[i, 7], g2.at[i, 15], s2.at[lax.rem(PIECES + i, RING), 11], r2s.at[i, 2], to_s).start()

    def from_sibling(i, groups):
        for group in groups:
            ref = g2.at[i, pl.ds(8, 4)] if group == 0 else g2.at[i, pl.ds(12, 3)] if group == 1 else g2.at[i, 15]
            arrived(ref, r2s.at[i, group])

    def drain2(i):
        for k in (0, 1, 2, 11):
            left(g2.at[i, 0], s2.at[lax.rem(PIECES + i, RING), k])
        for k in (3, 4):
            left(g2.at[i, 0, rows2, near2], s2.at[lax.rem(PIECES + i, RING), k])
        for k in (12, 13):
            left(g2.at[i, 0, rows2, far2], s2.at[lax.rem(PIECES + i, RING), k])
        for k in (5, 6, 8, 9):
            left(g2.at[i, 0, rows2, half2[0]], s2.at[lax.rem(PIECES + i, RING), k])
        left(g2.at[i, pl.ds(0, 4)], s2.at[lax.rem(PIECES + i, RING), 7])
        left(g2.at[i, pl.ds(4, 3)], s2.at[lax.rem(PIECES + i, RING), 10])

    def keep(q, slots, scores):
        for n, (p, k) in enumerate(slots):
            dx, dz = SLOTS[k]
            sx, sz = (1 - xh if dx else xh), lax.rem(z + dz, 4)
            row = pl.multiple_of(lax.rem(sz, 2) * 32 + (1 - c if p else c) * 16, 16)
            cs[lax.rem(q, 4), sx * 2 + sz // 2, pl.ds(row, 16), :] = scores[n * 16 : n * 16 + 16].astype(BF)

    every = [(p, k) for p in range(2) for k in range(8)]
    early = [(p, k) for p in range(2) for k in range(4)]
    late = [(p, k) for p in range(2) for k in range(4, 8)]

    def to_y(q):
        for d in (1, 2, 3):
            remote(cs.at[lax.rem(q, 4), lax.rem(y + d, 4)], yr.at[q, d - 1], ysend.at[lax.rem(q, 4), d - 1], ysem.at[q, d - 1],
                   to_lay[d, 0]).start()

    def over_y(q):
        total = cs[lax.rem(q, 4), y].astype(F32)
        for d in range(3):
            arrived(yr.at[q, d], ysem.at[q, d])
            left(yr.at[q, d], ysend.at[lax.rem(q, 4), d])
            total += yr[q, d].astype(F32)
        ysum[lax.rem(q, 4)] = total.reshape(2, 32, 512)
        xs[lax.rem(q, 4)] = ysum[lax.rem(q, 4), 1 - xl].astype(BF)
        remote(xs.at[lax.rem(q, 4)], xr.at[q], xsend.at[lax.rem(q, 4)], xsem.at[q], to_lay[0, 1]).start()

    def finish(q, total):
        for k in range(2):
            out[pl.ds(pl.multiple_of(k * 128 + q * 16, 16), 16), :] = total[k * 16 : k * 16 + 16]

    def over_x(q):
        arrived(xr.at[q], xsem.at[q])
        left(xr.at[q], xsend.at[lax.rem(q, 4)])
        finish(q, ysum[lax.rem(q, 4), xl] + xr[q].astype(F32))

    def main_head(q):
        rows = pl.ds(pl.multiple_of(q * 16, 16), 16)
        acc[1] = jnp.zeros((256, 512), F32)

        @pl.loop(0, PIECES // 2)
        def _(j):
            cols = pl.ds(pl.multiple_of(j * 1024, 1024), 1024)
            for l in (0, 1):
                lhs = g1[j * 2 + l, :, rows, :].reshape(256, 1024)
                acc[1] += lax.dot_general(lhs, bmat[l, :, cols], NT, preferred_element_type=F32)

        keep(q, every, acc[1])
        to_y(q)

    def product(l, lhs):
        return lax.dot_general(lhs, bmat[l], NT, preferred_element_type=F32)

    def main_item(n):
        l = lax.rem(n, 2)
        acc[0] = jnp.where(l == 0, jnp.zeros((256, 512), F32), acc[0]) + product(l, g2[n].reshape(256, 4096))

        @pl.when(l == 1)
        def _():
            q = HEAD // 16 + n // 2
            keep(q, every, acc[0])
            to_y(q)

    fetch(-1).wait()
    split_layers(0, write_a)
    fetch(1).start()
    prepare(0)
    pl.semaphore_wait(barrier, 11)

    end1, end2 = PIECES, PIECES + ITEMS

    @pl.loop(0, end2 + 3)
    def _(t):
        def during(start, stop, do, odd=None):
            on = (t >= start) & (t < stop)
            if odd is not None:
                on = on & (lax.rem(t, 2) == odd)
            pl.when(on)(do)

        def head_from_sibling():
            @pl.loop(0, PIECES)
            def _(p):
                for group in (0, 1):
                    arrived(g1.at[p, pl.ds(8 + 4 * group, 4)], r1s.at[p, group])

        during(RING, end1 + RING, lambda: drain1(t - RING))
        during(end1 + RING, end2 + RING, lambda: drain2(t - end1 - RING))
        during(0, end1, lambda: own1(t))
        during(end1, end2, lambda: own2(t - end1))
        during(1, end1 + 1, lambda: first1(t - 1))
        during(end1 + 1, end2 + 1, lambda: first2(t - end1 - 1))
        during(2, end1 + 2, lambda: second1(t - 2))
        during(end1 + 2, end2 + 2, lambda: second2(t - end1 - 2))

        def item():
            from_sibling(t - end1 - 4, (0, 1, 2))
            main_item(t - end1 - 4)

        first_main = end1 + 3
        heads = HEAD // 16
        during(first_main, first_main + 1, head_from_sibling)
        during(first_main, first_main + heads, lambda: main_head(t - first_main))
        during(end1 + 4, end2 + 3, item)
        during(first_main + 1, first_main + 1 + heads, lambda: over_y(t - first_main - 1))
        during(end1 + 6, end2 + 2, lambda: over_y(heads + (t - end1 - 6) // 2), end1 % 2)
        during(first_main + 2, first_main + 2 + heads, lambda: over_x(t - first_main - 2))
        during(end1 + 7, end2 + 3, lambda: over_x(heads + (t - end1 - 7) // 2), 1 - end1 % 2)
        during(3, end1 + 3, lambda: third1(t - 3))
        during(0, end1 - 1, lambda: prepare(t + 1))
        during(end1 - 1, end1 + 3, lambda: split_train(t - end1 + 1))
        during(end1 + 3, end2 + 2, lambda: third2(t - end1 - 3))

    i, q = ITEMS - 1, QUEUE - 1

    def last(k, slots):
        lhs = jnp.concatenate([g2[i, p + k : p + k + 4].reshape(64, 4096) for p in (0, 8)], axis=0)
        done = jnp.concatenate([acc[0, (p + k) * 16 : (p + k) * 16 + 64] for p in (0, 8)], axis=0)
        keep(q, slots, done + product(1, lhs))

    third2(i)

    def leave(k, first, rows, sem):
        part = pl.ds(k * 128 + first, rows)
        return pltpu.make_async_copy(out.at[part], result.at[part], osem.at[sem])

    for k in range(2):
        leave(k, 0, 96, k).start()
    from_sibling(i, (0,))
    last(0, early)

    from_sibling(i, (1, 2))
    last(4, late)
    mine = pl.ds(pl.multiple_of(xl * 32, 32), 32)
    yours = pl.ds(pl.multiple_of(32 - xl * 32, 32), 32)
    for n, (d, f) in enumerate(others):
        remote(cs.at[q % 4, lax.rem(y + d, 4), yours if f else mine], zr.at[n], zsend.at[n], zsem.at[n],
               to_lay[d, f]).start()
    for n in range(end2 + 3 - RING, end2):
        drain2(n - end1)
    over_y(q - 1)
    total = cs[q % 4, y, mine, :].astype(F32)
    for n in range(len(others)):
        arrived(zr.at[n], zsem.at[n])
        total += zr[n].astype(F32)
    finish(q, total)
    over_x(q - 1)
    for k in range(2):
        leave(k, 96, 32, 2 + k).start()
    for n in range(len(others)):
        left(zr.at[n], zsend.at[n])
    for k in range(2):
        leave(k, 0, 96, k).wait()
        leave(k, 96, 32, 2 + k).wait()


def body(train, test, inv_out, inv_in):
    vmem, hbm = pl.BlockSpec(memory_space=pltpu.VMEM), pl.BlockSpec(memory_space=pl.ANY)
    dma = pltpu.SemaphoreType.DMA
    return pl.pallas_call(
        kernel,
        out_shape=jax.ShapeDtypeStruct((256, 512), F32),
        in_specs=[hbm, hbm, vmem, vmem],
        out_specs=hbm,
        scratch_shapes=[
            pltpu.VMEM((256, 512), F32),
            dma((4,)),
            pltpu.VMEM((PIECES, 16, HEAD, 1024), BF),
            pltpu.VMEM((ITEMS, 16, ROWS, 4096), BF),
            pltpu.VMEM((2, 512, 4096), BF),
            pltpu.VMEM((2, 256, 4096), BF),
            pltpu.VMEM((2, 128, 4096), BF),
            pltpu.VMEM((4096, PART), BF),
            pltpu.VMEM((4, 4, 64, 512), BF),
            pltpu.VMEM((QUEUE - 1, 3, 64, 512), BF),
            pltpu.VMEM((4, 32, 512), BF),
            pltpu.VMEM((QUEUE - 1, 32, 512), BF),
            pltpu.VMEM((4, 2, 32, 512), F32),
            pltpu.VMEM((7, 32, 512), BF),
            pltpu.VMEM((2, 256, 512), F32),
            dma((PIECES, 5)),
            dma((PIECES, 2, 2)),
            dma((PIECES, 2)),
            dma((PIECES, 2)),
            dma((ITEMS, 5)),
            dma((ITEMS, 2, 2)),
            dma((ITEMS, 2)),
            dma((ITEMS, 3)),
            dma((RING, 14)),
            dma((QUEUE - 1, 3)),
            dma((4, 3)),
            dma((QUEUE - 1,)),
            dma((4,)),
            dma((7,)),
            dma((7,)),
            dma((2,)),
        ],
        compiler_params=pltpu.CompilerParams(
            collective_id=0, has_side_effects=True, vmem_limit_bytes=62 * 2**20
        ),
        cost_estimate=pl.CostEstimate(flops=26 * 10**9, bytes_accessed=12 * 2**20, transcendentals=0),
    )(train, test, inv_out, inv_in)


def solution(mesh):
    return jax.shard_map(
        body,
        mesh=mesh,
        in_specs=(P("ex", "lay", None), P("ex", "lay", None), P("lay", None, None), P("lay", None, None)),
        out_specs=P("lay", "ex"),
        check_vma=False,
    )
```
